32 devices in a mesh: blk: 16 (over z, y, x), layer: 2 (over core).
Axes of the slice: x: 2, y: 2, z: 4, core: 2. Of those that a mesh axis runs over, the one named last changes fastest.
Arguments:
- train_factors: bfloat16 [192, 2, 2, 64, 1024], P('blk', 'layer'), may hold values from -0.29882812 to 0.29882812
- val_factors: bfloat16 [64, 2, 2, 64, 1024], P('blk', 'layer'), may hold values from -0.29882812 to 0.29882812
Outputs:
- scores: float32 [192, 3, 4], P('blk')
The draws below stay inside these ranges and needn't reach their ends.
All inputs are finite; a program needn't handle non-finite values.
Results may differ from the reference program's by a relative error of at most 0.0003.
Values may be sent and summed in bfloat16 or wider, within the bound.
No kernel may reach another device: no remote copies, remote signals or barrier semaphores. Data moves between devices by JAX's collectives and lax.ppermute only.
A program may use at most 64 MiB of HBM per device.

```python
import jax
import jax.numpy as jnp
from jax import lax

R = 1024
TOK = 64
TRAIN_DEV = 12
VAL_DEV = 4
HOPS = 3
TRAIN = 192
VAL = 64
LAYERS = 2
N_BLK = 16


def block_scale(own_key, dims, pieces, low, top_value):
    def one(position, shards_of):
        steps = jax.random.uniform(jax.random.fold_in(jax.random.fold_in(own_key, 6), position), (shards_of,), jnp.float32, low / len(pieces), top_value / len(pieces))
        return jnp.repeat(jnp.exp(steps), dims[position] // shards_of).reshape((-1,) + (1,) * (len(dims) - position - 1))

    factor_of = one(*pieces[0])
    for cut in pieces[1:]:
        factor_of = factor_of * one(*cut)
    return factor_of


def centred(rng, extent, deviation, limit, split=(), kind=jnp.bfloat16):
    level = block_scale(rng, extent, split, -0.22, 0.18) if split else 1.0
    values = jax.random.normal(rng, extent, jnp.float32) * deviation * level
    return jnp.minimum(jnp.maximum(values, -limit), limit).astype(kind)


def setup_inputs(seed: int = 0) -> dict:
    seeds = jax.random.split(jax.random.key(seed), 3)
    return {
        "train_factors": centred(seeds[0], (TRAIN, LAYERS, 2, TOK, R), 0.05, 0.29882812, ((0, 16), (1, 2))),
        "val_factors": centred(seeds[1], (VAL, LAYERS, 2, TOK, R), 0.05, 0.29882812, ((0, 16), (1, 2))),
    }


def pair_scores(train, val):
    train_f = train.astype(jnp.float32)
    val_f = val.astype(jnp.float32)
    act_gram = jnp.einsum('iltr,jlsr->ijlts', train_f[:, :, 0], val_f[:, :, 0])
    grad_gram = jnp.einsum('iltr,jlsr->ijlts', train_f[:, :, 1], val_f[:, :, 1])
    return jnp.sum(act_gram * grad_gram, axis=(2, 3, 4))


def reference(train_factors, val_factors):
    train_blocks = train_factors.reshape((N_BLK, TRAIN_DEV) + train_factors.shape[1:])
    val_blocks = val_factors.reshape((N_BLK, VAL_DEV) + val_factors.shape[1:])

    def one_block(index):
        train = lax.dynamic_index_in_dim(train_blocks, index, 0, keepdims=False)
        rows = []
        for hop in range(HOPS):
            source = ((index - hop) % N_BLK).astype(jnp.int32)
            val = lax.dynamic_index_in_dim(val_blocks, source, 0, keepdims=False)
            rows.append(pair_scores(train, val))
        return jnp.stack(rows, axis=1)

    result = lax.map(one_block, jnp.arange(N_BLK, dtype=jnp.int32))
    return result.reshape((N_BLK * TRAIN_DEV, HOPS, VAL_DEV))
```

```python
import functools

import jax
import jax.numpy as jnp
from jax import lax
from jax.experimental import pallas as pl
from jax.experimental.pallas import tpu as pltpu
from jax.sharding import PartitionSpec as P

GROUP = 4


def permuted(block, axis, distance):
    size = lax.axis_size(axis)
    return lax.ppermute(block, axis, [(i, (i + distance) % size) for i in range(size)])


def to_partner(block, axis, parity):
    size = lax.axis_size(axis)
    return lax.ppermute(block, axis, [(i, i ^ 1) for i in range(size) if i % 2 == parity])


def score_kernel(first_val, odd_ref, train_ref, *refs):
    *part_refs, out_ref = refs
    block_ref = part_refs.pop(0) if first_val is not None else None
    examples, layers, _, tokens, features = train_ref.shape
    rows = out_ref.shape[1] * tokens
    group = GROUP if examples % GROUP == 0 else 1

    def val_rows(layer, index):
        parts, start = [], first_val
        for ref in part_refs:
            part = ref[:, layer, index]
            if block_ref is not None:
                part = jnp.where(odd_ref[0] == 1, block_ref[start : start + ref.shape[0], layer, index], part)
                start += ref.shape[0]
            parts.append(part.reshape(ref.shape[0] * tokens, features))
        return jnp.concatenate(parts, axis=0) if len(parts) > 1 else parts[0]

    vals = [[val_rows(layer, index) for index in range(2)] for layer in range(layers)]

    def gram(layer, index, first):
        train = train_ref[first : first + group, layer, index].reshape(group * tokens, features)
        return lax.dot_general(
            train, vals[layer][index], (((1,), (1,)), ((), ())), preferred_element_type=jnp.float32
        )

    sums = []
    for first in range(0, examples, group):
        product = 0.0
        for layer in range(layers):
            product = product + gram(layer, 0, first) * gram(layer, 1, first)
        sums.append(jnp.sum(product.reshape(group, tokens, rows), axis=1))
    by_token = jnp.concatenate(sums, axis=0)
    column = lax.broadcasted_iota(jnp.int32, by_token.shape, 1) // tokens
    scores = [
        jnp.sum(jnp.where(column == v, by_token, 0.0), axis=1, keepdims=True)
        for v in range(rows // tokens)
    ]
    out_ref[...] = jnp.concatenate(scores, axis=1)


def pair_scores(odd, train, parts, block=None, first_val=None):
    count = sum(part.shape[0] for part in parts)
    examples, layers, _, tokens, features = train.shape
    vmem = pl.BlockSpec(memory_space=pltpu.VMEM)
    operands = ([] if block is None else [block]) + list(parts)
    return pl.pallas_call(
        functools.partial(score_kernel, first_val),
        out_shape=jax.ShapeDtypeStruct((examples, count), jnp.float32),
        in_specs=[pl.BlockSpec(memory_space=pltpu.SMEM)] + [vmem] * (1 + len(operands)),
        out_specs=vmem,
        compiler_params=pltpu.CompilerParams(vmem_limit_bytes=16 << 20),
        cost_estimate=pl.CostEstimate(
            flops=4 * examples * count * layers * tokens * tokens * features,
            bytes_accessed=2 * (examples + count) * layers * 2 * tokens * features,
            transcendentals=0,
        ),
    )(odd, train, *operands)


def local(train_factors, val_factors):
    size = lax.axis_size("blk")
    odd = (lax.axis_index("blk") % 2).astype(jnp.int32).reshape(1)
    score = functools.partial(pair_scores, odd, train_factors)
    second = [
        permuted(val_factors[c : c + 1], "blk", 2) for c in range(val_factors.shape[0])
    ]
    if size % 2 == 0:
        block = to_partner(val_factors, "blk", 0)
        parts = [to_partner(part, "blk", 1) for part in second]
        first = [score(parts[:-1], block, 0), score(parts[-1:], block, len(parts) - 1)]
    else:
        first = [score([permuted(val_factors, "blk", 1)])]
    rows = [score([val_factors]), jnp.concatenate(first, axis=1), score(second)]
    return lax.psum(jnp.stack(rows, axis=1), "layer")


def solution(mesh):
    return jax.shard_map(
        local,
        mesh=mesh,
        in_specs=(P("blk", "layer", None, None, None), P("blk", "layer", None, None, None)),
        out_specs=P("blk", None, None),
        check_vma=False,
    )
```

```python
import functools

import jax
import jax.numpy as jnp
from jax import lax
from jax.experimental import pallas as pl
from jax.experimental.pallas import tpu as pltpu
from jax.sharding import PartitionSpec as P

CUTS = 4
GROUP = 4

VMEM = pl.BlockSpec(memory_space=pltpu.VMEM)
SMEM = pl.BlockSpec(memory_space=pltpu.SMEM)
HBM = pl.BlockSpec(memory_space=pltpu.HBM)
DMA = pltpu.SemaphoreType.DMA


def permuted(block, axis, target):
    size = lax.axis_size(axis)
    return lax.ppermute(block, axis, [(i, target(i) % size) for i in range(size)])


def call(kernel, out_shape, specs, operands, flops=0, scratch=(), vmem=16 << 20):
    shapes = list(operands) + jax.tree.leaves(out_shape)
    return pl.pallas_call(
        kernel,
        out_shape=out_shape,
        in_specs=specs,
        out_specs=jax.tree.map(lambda _: VMEM, out_shape),
        scratch_shapes=scratch,
        compiler_params=pltpu.CompilerParams(vmem_limit_bytes=vmem),
        cost_estimate=pl.CostEstimate(
            flops=flops,
            bytes_accessed=sum(x.size * x.dtype.itemsize for x in shapes),
            transcendentals=0,
        ),
    )(*operands)


def groups(train_ref):
    examples = train_ref.shape[0]
    size = GROUP if examples % GROUP == 0 else 1
    return [slice(first, first + size) for first in range(0, examples, size)]


def gram(train_ref, val_refs, layer, index, group, start=0):
    total = 0.0
    for ref in val_refs:
        depth = ref.shape[-1]
        train = train_ref[group, layer, index, :, start : start + depth].reshape(-1, depth)
        val = ref[:, layer, index].reshape(-1, depth)
        total = total + lax.dot_general(
            train, val, (((1,), (1,)), ((), ())), preferred_element_type=jnp.float32
        )
        start += depth
    return total


def token_sums(product, tokens):
    return jnp.sum(product.reshape(-1, tokens, product.shape[-1]), axis=1)


def example_sums(by_token, tokens):
    count = by_token.shape[-1] // tokens
    shape = (count, by_token.shape[-1])
    token = lax.broadcasted_iota(jnp.int32, shape, 1) // tokens
    mine = (token == lax.broadcasted_iota(jnp.int32, shape, 0)).astype(jnp.float32)
    return lax.dot_general(
        mine, by_token, (((1,), (1,)), ((), ())),
        precision=lax.Precision.HIGHEST, preferred_element_type=jnp.float32,
    )


def scores(train_ref, val_refs, ready=lambda group: None):
    layers, tokens = train_ref.shape[1], train_ref.shape[3]
    sums = []
    for group in groups(train_ref):
        ready(group)
        product = 0.0
        for layer in range(layers):
            product = product + gram(train_ref, val_refs, layer, 0, group) * gram(
                train_ref, val_refs, layer, 1, group
            )
        sums.append(token_sums(product, tokens))
    return example_sums(jnp.concatenate(sums, axis=0), tokens)


def own_kernel(train_hbm, val_hbm, *refs):
    *part_refs, out_ref, train_ref, val_ref, train_sems, val_sem = refs
    val_copy = pltpu.make_async_copy(val_hbm, val_ref, val_sem)
    val_copy.start()
    train_copies = {
        group.start: pltpu.make_async_copy(train_hbm.at[group], train_ref.at[group], train_sems.at[n])
        for n, group in enumerate(groups(train_ref))
    }
    for copy in train_copies.values():
        copy.start()
    val_copy.wait()
    for c, ref in enumerate(part_refs, 1):
        depth = ref.shape[-1]
        ref[...] = val_ref[..., c * depth : (c + 1) * depth]
    out_ref[...] = scores(train_ref, [val_ref], lambda group: train_copies[group.start].wait())


def pick_kernel(odd_ref, even_ref, far_ref, out_ref):
    @pl.when(odd_ref[0] == 1)
    def _():
        out_ref[...] = far_ref[...]

    @pl.when(odd_ref[0] == 0)
    def _():
        out_ref[...] = even_ref[...]


def middle_kernel(cuts, train_ref, *refs):
    second_refs, first_refs, (grams_ref, out_ref) = refs[:cuts], refs[cuts:-2], refs[-2:]
    layers, tokens = train_ref.shape[1], train_ref.shape[3]
    out_ref[...] = scores(train_ref, second_refs)
    for layer in range(layers):
        for index in range(2):
            for group in groups(train_ref):
                rows = slice(group.start * tokens, group.stop * tokens)
                grams_ref[layer, index, rows] = gram(train_ref, first_refs, layer, index, group)


def last_kernel(train_ref, part_ref, grams_ref, own_ref, second_ref, out_ref):
    layers, tokens, features = train_ref.shape[1], train_ref.shape[3], train_ref.shape[4]
    start = features - part_ref.shape[-1]
    sums = []
    for group in groups(train_ref):
        rows = slice(group.start * tokens, group.stop * tokens)
        product = 0.0
        for layer in range(layers):
            act, grad = (
                grams_ref[layer, index, rows] + gram(train_ref, [part_ref], layer, index, group, start)
                for index in range(2)
            )
            product = product + act * grad
        sums.append(token_sums(product, tokens))
    out_ref[0] = own_ref[...]
    out_ref[1] = example_sums(jnp.concatenate(sums, axis=0), tokens)
    out_ref[2] = second_ref[...]


def local(train, val):
    examples, layers, _, tokens, features = train.shape
    count = val.shape[0]
    cuts = CUTS if features % (CUTS * 128) == 0 else 1
    depth = features // cuts
    work = 4 * examples * count * layers * tokens * tokens * features
    part = jax.ShapeDtypeStruct(val.shape[:-1] + (depth,), val.dtype)
    rows = jax.ShapeDtypeStruct((count, examples), jnp.float32)
    grams = jax.ShapeDtypeStruct((layers, 2, examples * tokens, count * tokens), jnp.float32)
    odd = (lax.axis_index("blk") % 2).astype(jnp.int32).reshape(1)

    *parts, own = call(
        own_kernel,
        [part] * (cuts - 1) + [rows],
        [HBM, HBM],
        [train, val],
        work,
        [pltpu.VMEM(train.shape, train.dtype), pltpu.VMEM(val.shape, val.dtype), DMA((examples,)), DMA],
        vmem=62 << 20,
    )
    parts = [val[..., :depth]] + parts
    second = [permuted(x, "blk", lambda i: i + 2) for x in parts]
    if lax.axis_size("blk") % 2 == 0:
        picked = [call(pick_kernel, part, [SMEM, VMEM, VMEM], [odd, x, y]) for x, y in zip(parts, second)]
        first = [permuted(x, "blk", lambda i: i ^ 1) for x in picked]
    else:
        first = [permuted(x, "blk", lambda i: i + 1) for x in parts]
    operands = [train] + second + first[:-1]
    sums, far = call(
        functools.partial(middle_kernel, cuts), [grams, rows], [VMEM] * len(operands), operands, 2 * work
    )
    out = jax.ShapeDtypeStruct((3,) + rows.shape, jnp.float32)
    partial_rows = call(last_kernel, out, [VMEM] * 5, [train, first[-1], sums, own, far], work // cuts)
    return lax.psum(partial_rows, "layer").transpose(2, 0, 1)


def solution(mesh):
    return jax.shard_map(
        local,
        mesh=mesh,
        in_specs=(P("blk", "layer", None, None, None), P("blk", "layer", None, None, None)),
        out_specs=P("blk", None, None),
        check_vma=False,
    )
```

```python
import functools

import jax
import jax.numpy as jnp
from jax import lax
from jax.experimental import pallas as pl
from jax.experimental.pallas import tpu as pltpu
from jax.sharding import PartitionSpec as P

CUTS = 4
GROUP = 4

VMEM = pl.BlockSpec(memory_space=pltpu.VMEM)
SMEM = pl.BlockSpec(memory_space=pltpu.SMEM)
HBM = pl.BlockSpec(memory_space=pltpu.HBM)
DMA = pltpu.SemaphoreType.DMA


def permuted(block, axis, target, sends=lambda i: True):
    size = lax.axis_size(axis)
    return lax.ppermute(block, axis, [(i, target(i) % size) for i in range(size) if sends(i)])


def call(kernel, out_shape, specs, operands, flops=0, scratch=(), vmem=16 << 20):
    shapes = list(operands) + jax.tree.leaves(out_shape)
    return pl.pallas_call(
        kernel,
        out_shape=out_shape,
        in_specs=specs,
        out_specs=jax.tree.map(lambda _: VMEM, out_shape),
        scratch_shapes=scratch,
        compiler_params=pltpu.CompilerParams(vmem_limit_bytes=vmem),
        cost_estimate=pl.CostEstimate(
            flops=flops,
            bytes_accessed=sum(x.size * x.dtype.itemsize for x in shapes),
            transcendentals=0,
        ),
    )(*operands)


def groups(train_ref):
    examples = train_ref.shape[0]
    size = GROUP if examples % GROUP == 0 else 1
    return [slice(first, first + size) for first in range(0, examples, size)]


def gram(train_ref, val_refs, layer, index, group, start=0):
    total = 0.0
    for ref in val_refs:
        depth = ref.shape[-1]
        train = train_ref[group, layer, index, :, start : start + depth].reshape(-1, depth)
        val = ref[:, layer, index].reshape(-1, depth)
        total = total + lax.dot_general(
            train, val, (((1,), (1,)), ((), ())), preferred_element_type=jnp.float32
        )
        start += depth
    return total


def token_sums(product, tokens):
    return jnp.sum(product.reshape(-1, tokens, product.shape[-1]), axis=1)


def example_sums(by_token, tokens):
    count = by_token.shape[-1] // tokens
    shape = (count, by_token.shape[-1])
    token = lax.broadcasted_iota(jnp.int32, shape, 1) // tokens
    mine = (token == lax.broadcasted_iota(jnp.int32, shape, 0)).astype(jnp.float32)
    return lax.dot_general(
        mine, by_token, (((1,), (1,)), ((), ())),
        precision=lax.Precision.HIGHEST, preferred_element_type=jnp.float32,
    )


def scores(train_ref, val_refs):
    layers, tokens = train_ref.shape[1], train_ref.shape[3]
    sums = []
    for group in groups(train_ref):
        product = 0.0
        for layer in range(layers):
            product = product + gram(train_ref, val_refs, layer, 0, group) * gram(
                train_ref, val_refs, layer, 1, group
            )
        sums.append(token_sums(product, tokens))
    return example_sums(jnp.concatenate(sums, axis=0), tokens)


def cut_kernel(val_ref, *part_refs):
    for c, ref in enumerate(part_refs, 1):
        depth = ref.shape[-1]
        ref[...] = val_ref[..., c * depth : (c + 1) * depth]


def scores_kernel(train_ref, *refs):
    *val_refs, out_ref = refs
    out_ref[...] = scores(train_ref, val_refs)


def by_parity(even, odd):
    parity = lax.rem(lax.axis_index("blk"), 2)
    pl.when(parity == 0)(even)
    pl.when(parity == 1)(odd)


def pick_kernel(even_ref, odd_ref, out_ref):
    def put(ref):
        out_ref[...] = ref[...]

    by_parity(lambda: put(even_ref), lambda: put(odd_ref))


def sums_kernel(train_ref, *refs):
    *part_refs, grams_ref = refs
    layers, tokens = train_ref.shape[1], train_ref.shape[3]
    for layer in range(layers):
        for index in range(2):
            for group in groups(train_ref):
                rows = slice(group.start * tokens, group.stop * tokens)
                grams_ref[layer, index, rows] = gram(train_ref, part_refs, layer, index, group)


def last_kernel(train_ref, even_ref, odd_ref, grams_ref, own_ref, second_ref, out_ref):
    layers, tokens, features = train_ref.shape[1], train_ref.shape[3], train_ref.shape[4]

    def finish(part_ref):
        start = features - part_ref.shape[-1]
        sums = []
        for group in groups(train_ref):
            rows = slice(group.start * tokens, group.stop * tokens)
            product = 0.0
            for layer in range(layers):
                act, grad = (
                    grams_ref[layer, index, rows] + gram(train_ref, [part_ref], layer, index, group, start)
                    for index in range(2)
                )
                product = product + act * grad
            sums.append(token_sums(product, tokens))
        out_ref[1] = example_sums(jnp.concatenate(sums, axis=0), tokens)

    out_ref[0] = own_ref[...]
    out_ref[2] = second_ref[...]
    by_parity(lambda: finish(even_ref), lambda: finish(odd_ref))


def local(train, val):
    examples, layers, _, tokens, features = train.shape
    count = val.shape[0]
    cuts = CUTS
    depth = features // cuts
    work = 4 * examples * count * layers * tokens * tokens * features
    part = jax.ShapeDtypeStruct(val.shape[:-1] + (depth,), val.dtype)
    rows = jax.ShapeDtypeStruct((count, examples), jnp.float32)
    grams = jax.ShapeDtypeStruct((layers, 2, examples * tokens, count * tokens), jnp.float32)

    parts = [val[..., :depth], *call(cut_kernel, [part] * (cuts - 1), [VMEM], [val])]
    second = [permuted(x, "blk", lambda i: i + 2) for x in parts]
    last = permuted(parts[-1], "blk", lambda i: i ^ 1)
    picked = [call(pick_kernel, part, [VMEM] * 2, [x, y]) for x, y in zip(parts[:-1], second)]
    first = [permuted(x, "blk", lambda i: i ^ 1) for x in picked]
    far_last = permuted(last, "blk", lambda i: i + 2, lambda i: i % 2 == 0)

    own = call(scores_kernel, rows, [VMEM] * 2, [train, val], work)
    far = call(scores_kernel, rows, [VMEM] * (1 + cuts), [train] + second, work)
    sums = call(sums_kernel, grams, [VMEM] * (1 + len(first)), [train] + first, work)
    out = jax.ShapeDtypeStruct((3,) + rows.shape, jnp.float32)
    operands = [train, far_last, last, sums, own, far]
    partial_rows = call(last_kernel, out, [VMEM] * len(operands), operands, work // cuts)
    return lax.psum(partial_rows, "layer").transpose(2, 0, 1)


def solution(mesh):
    return jax.shard_map(
        local,
        mesh=mesh,
        in_specs=(P("blk", "layer", None, None, None), P("blk", "layer", None, None, None)),
        out_specs=P("blk", None, None),
        check_vma=False,
    )
```

```python
import functools

import jax
import jax.numpy as jnp
from jax import lax
from jax.experimental import pallas as pl
from jax.experimental.pallas import tpu as pltpu
from jax.sharding import PartitionSpec as P

CUTS = 4
GROUP = 4

VMEM = pl.BlockSpec(memory_space=pltpu.VMEM)


def permuted(block, axis, target, sends=lambda i: True):
    size = lax.axis_size(axis)
    return lax.ppermute(block, axis, [(i, target(i) % size) for i in range(size) if sends(i)])


def call(kernel, out_shape, specs, operands, flops=0, scratch=(), vmem=16 << 20):
    shapes = list(operands) + jax.tree.leaves(out_shape)
    return pl.pallas_call(
        kernel,
        out_shape=out_shape,
        in_specs=specs,
        out_specs=jax.tree.map(lambda _: VMEM, out_shape),
        scratch_shapes=scratch,
        compiler_params=pltpu.CompilerParams(vmem_limit_bytes=vmem),
        cost_estimate=pl.CostEstimate(
            flops=flops,
            bytes_accessed=sum(x.size * x.dtype.itemsize for x in shapes),
            transcendentals=0,
        ),
    )(*operands)


def groups(train_ref):
    examples = train_ref.shape[0]
    size = GROUP if examples % GROUP == 0 else 1
    return [slice(first, first + size) for first in range(0, examples, size)]


def gram(train_ref, val_refs, layer, index, group, start=0):
    total = 0.0
    for ref in val_refs:
        depth = ref.shape[-1]
        train = train_ref[group, layer, index, :, start : start + depth].reshape(-1, depth)
        val = ref[:, layer, index].reshape(-1, depth)
        total = total + lax.dot_general(
            train, val, (((1,), (1,)), ((), ())), preferred_element_type=jnp.float32
        )
        start += depth
    return total


def token_sums(product, tokens):
    return jnp.sum(product.reshape(-1, tokens, product.shape[-1]), axis=1)


def example_sums(by_token, tokens):
    count = by_token.shape[-1] // tokens
    shape = (count, by_token.shape[-1])
    token = lax.broadcasted_iota(jnp.int32, shape, 1) // tokens
    mine = (token == lax.broadcasted_iota(jnp.int32, shape, 0)).astype(jnp.float32)
    return lax.dot_general(
        mine, by_token, (((1,), (1,)), ((), ())),
        precision=lax.Precision.HIGHEST, preferred_element_type=jnp.float32,
    )


def scores(train_ref, val_refs):
    layers, tokens = train_ref.shape[1], train_ref.shape[3]
    sums = []
    for group in groups(train_ref):
        product = 0.0
        for layer in range(layers):
            product = product + gram(train_ref, val_refs, layer, 0, group) * gram(
                train_ref, val_refs, layer, 1, group
            )
        sums.append(token_sums(product, tokens))
    return example_sums(jnp.concatenate(sums, axis=0), tokens)


def cut_kernel(val_ref, *part_refs):
    for c, ref in enumerate(part_refs, 1):
        depth = ref.shape[-1]
        ref[...] = val_ref[..., c * depth : (c + 1) * depth]


def scores_kernel(train_ref, *refs):
    *val_refs, out_ref = refs
    out_ref[...] = scores(train_ref, val_refs)


def by_parity(even, odd):
    parity = lax.rem(lax.axis_index("blk"), 2)
    pl.when(parity == 0)(even)
    pl.when(parity == 1)(odd)


def pick_kernel(even_ref, odd_ref, *refs):
    *next_ref, out_ref, copy_ref = refs if len(refs) == 3 else refs + (None,)

    def put(ref):
        out_ref[...] = ref[...]

    by_parity(lambda: put(even_ref), lambda: put(odd_ref))
    if next_ref:
        copy_ref[...] = next_ref[0][...]


def grams_kernel(train_ref, *refs):
    *part_refs, out_ref = refs
    layers, tokens = train_ref.shape[1], train_ref.shape[3]
    for layer in range(layers):
        for index in range(2):
            for group in groups(train_ref):
                rows = slice(group.start * tokens, group.stop * tokens)
                out_ref[layer, index, rows] = gram(train_ref, part_refs, layer, index, group)


def add_kernel(train_ref, even_ref, odd_ref, grams_ref, _, out_ref):
    layers, tokens, features = train_ref.shape[1], train_ref.shape[3], train_ref.shape[4]

    def add(part_ref):
        start = features - part_ref.shape[-1]
        for layer in range(layers):
            for index in range(2):
                for group in groups(train_ref):
                    rows = slice(group.start * tokens, group.stop * tokens)
                    out_ref[layer, index, rows] = grams_ref[layer, index, rows] + gram(
                        train_ref, [part_ref], layer, index, group, start
                    )

    by_parity(lambda: add(even_ref), lambda: add(odd_ref))


def last_kernel(start, train_ref, part_ref, grams_ref, own_ref, second_ref, out_ref):
    layers, tokens = train_ref.shape[1], train_ref.shape[3]
    sums = []
    for group in groups(train_ref):
        rows = slice(group.start * tokens, group.stop * tokens)
        product = 0.0
        for layer in range(layers):
            act, grad = (
                grams_ref[layer, index, rows] + gram(train_ref, [part_ref], layer, index, group, start)
                for index in range(2)
            )
            product = product + act * grad
        sums.append(token_sums(product, tokens))
    out_ref[0] = own_ref[...]
    out_ref[1] = example_sums(jnp.concatenate(sums, axis=0), tokens)
    out_ref[2] = second_ref[...]


def local(train, val):
    examples, layers, _, tokens, features = train.shape
    count = val.shape[0]
    cuts = CUTS
    depth = features // cuts
    work = 4 * examples * count * layers * tokens * tokens * features
    part = jax.ShapeDtypeStruct(val.shape[:-1] + (depth,), val.dtype)
    rows = jax.ShapeDtypeStruct((count, examples), jnp.float32)
    grams = jax.ShapeDtypeStruct((layers, 2, examples * tokens, count * tokens), jnp.float32)

    parts = [val[..., :depth], *call(cut_kernel, [part] * (cuts - 1), [VMEM], [val])]
    last = permuted(parts[-1], "blk", lambda i: i + (1, -1, 1, 3)[i % 4])
    second = [permuted(x, "blk", lambda i: i + 2) for x in parts[:2]]
    first = []
    for c in range(cuts - 1):
        operands = [parts[c], second[c]] + parts[c + 2 : c + 3]
        picked, *later = call(pick_kernel, [part] * (len(operands) - 1), [VMEM] * len(operands), operands)
        second += [permuted(x, "blk", lambda i: i + 2) for x in later]
        first.append(permuted(picked, "blk", lambda i: i ^ 1))
    far_last = permuted(last, "blk", lambda i: i ^ 2, lambda i: i % 2 == 0)

    own = call(scores_kernel, rows, [VMEM] * 2, [train, val], work)
    far = call(scores_kernel, rows, [VMEM] * (1 + cuts), [train] + second, work)
    sums = call(grams_kernel, grams, [VMEM] * len(first), [train] + first[:-1], work // 2)
    sums = call(add_kernel, grams, [VMEM] * 5, [train, far_last, last, sums, far], work // cuts)
    out = jax.ShapeDtypeStruct((3,) + rows.shape, jnp.float32)
    kernel = functools.partial(last_kernel, depth * (cuts - 2))
    partial_rows = call(kernel, out, [VMEM] * 5, [train, first[-1], sums, own, far], work // cuts)
    return lax.psum(partial_rows, "layer").transpose(2, 0, 1)


def solution(mesh):
    return jax.shard_map(
        local,
        mesh=mesh,
        in_specs=(P("blk", "layer", None, None, None), P("blk", "layer", None, None, None)),
        out_specs=P("blk", None, None),
        check_vma=False,
    )
```

```python
import functools

import jax
import jax.numpy as jnp
from jax import lax
from jax.experimental import pallas as pl
from jax.experimental.pallas import tpu as pltpu
from jax.sharding import PartitionSpec as P

CUTS = 4
GROUP = 4

VMEM = pl.BlockSpec(memory_space=pltpu.VMEM)


def permuted(block, axis, target, sends=lambda i: True):
    size = lax.axis_size(axis)
    return lax.ppermute(block, axis, [(i, target(i) % size) for i in range(size) if sends(i)])


def call(kernel, out_shape, specs, operands, flops=0, scratch=(), vmem=16 << 20):
    shapes = list(operands) + jax.tree.leaves(out_shape)
    return pl.pallas_call(
        kernel,
        out_shape=out_shape,
        in_specs=specs,
        out_specs=jax.tree.map(lambda _: VMEM, out_shape),
        scratch_shapes=scratch,
        compiler_params=pltpu.CompilerParams(vmem_limit_bytes=vmem),
        cost_estimate=pl.CostEstimate(
            flops=flops,
            bytes_accessed=sum(x.size * x.dtype.itemsize for x in shapes),
            transcendentals=0,
        ),
    )(*operands)


def groups(train_ref):
    examples = train_ref.shape[0]
    size = GROUP if examples % GROUP == 0 else 1
    return [slice(first, first + size) for first in range(0, examples, size)]


def gram(train_ref, val_refs, layer, index, group, start=0):
    total = 0.0
    for ref in val_refs:
        depth = ref.shape[-1]
        train = train_ref[group, layer, index, :, start : start + depth].reshape(-1, depth)
        val = ref[:, layer, index].reshape(-1, depth)
        total = total + lax.dot_general(
            train, val, (((1,), (1,)), ((), ())), preferred_element_type=jnp.float32
        )
        start += depth
    return total


def token_sums(product, tokens):
    return jnp.sum(product.reshape(-1, tokens, product.shape[-1]), axis=1)


def example_sums(by_token, tokens):
    count = by_token.shape[-1] // tokens
    shape = (count, by_token.shape[-1])
    token = lax.broadcasted_iota(jnp.int32, shape, 1) // tokens
    mine = (token == lax.broadcasted_iota(jnp.int32, shape, 0)).astype(jnp.float32)
    return lax.dot_general(
        mine, by_token, (((1,), (1,)), ((), ())),
        precision=lax.Precision.HIGHEST, preferred_element_type=jnp.float32,
    )


def scores(train_ref, val_refs):
    layers, tokens = train_ref.shape[1], train_ref.shape[3]
    sums = []
    for group in groups(train_ref):
        product = 0.0
        for layer in range(layers):
            product = product + gram(train_ref, val_refs, layer, 0, group) * gram(
                train_ref, val_refs, layer, 1, group
            )
        sums.append(token_sums(product, tokens))
    return example_sums(jnp.concatenate(sums, axis=0), tokens)


def cut_kernel(val_ref, *part_refs):
    for c, ref in enumerate(part_refs, 1):
        depth = ref.shape[-1]
        ref[...] = val_ref[..., c * depth : (c + 1) * depth]


def scores_kernel(train_ref, *refs):
    *val_refs, out_ref = refs
    out_ref[...] = scores(train_ref, val_refs)


def by_parity(even, odd):
    parity = lax.rem(lax.axis_index("blk"), 2)
    pl.when(parity == 0)(even)
    pl.when(parity == 1)(odd)


def pick_kernel(even_ref, odd_ref, out_ref):
    def put(ref):
        out_ref[...] = ref[...]

    by_parity(lambda: put(even_ref), lambda: put(odd_ref))


def grams_kernel(train_ref, *refs):
    *part_refs, out_ref = refs
    layers, tokens = train_ref.shape[1], train_ref.shape[3]
    for layer in range(layers):
        for index in range(2):
            for group in groups(train_ref):
                rows = slice(group.start * tokens, group.stop * tokens)
                out_ref[layer, index, rows] = gram(train_ref, part_refs, layer, index, group)


def add_kernel(train_ref, even_ref, odd_ref, grams_ref, _, out_ref):
    layers, tokens, features = train_ref.shape[1], train_ref.shape[3], train_ref.shape[4]

    def add(part_ref):
        start = features - part_ref.shape[-1]
        for layer in range(layers):
            for index in range(2):
                for group in groups(train_ref):
                    rows = slice(group.start * tokens, group.stop * tokens)
                    out_ref[layer, index, rows] = grams_ref[layer, index, rows] + gram(
                        train_ref, [part_ref], layer, index, group, start
                    )

    by_parity(lambda: add(even_ref), lambda: add(odd_ref))


def last_kernel(start, train_ref, part_ref, grams_ref, own_ref, second_ref, out_ref):
    layers, tokens = train_ref.shape[1], train_ref.shape[3]
    sums = []
    for group in groups(train_ref):
        rows = slice(group.start * tokens, group.stop * tokens)
        product = 0.0
        for layer in range(layers):
            act, grad = (
                grams_ref[layer, index, rows] + gram(train_ref, [part_ref], layer, index, group, start)
                for index in range(2)
            )
            product = product + act * grad
        sums.append(token_sums(product, tokens))
    out_ref[0] = own_ref[...]
    out_ref[1] = example_sums(jnp.concatenate(sums, axis=0), tokens)
    out_ref[2] = second_ref[...]


def local(train, val):
    examples, layers, _, tokens, features = train.shape
    count = val.shape[0]
    cuts = CUTS
    depth = features // cuts
    work = 4 * examples * count * layers * tokens * tokens * features
    part = jax.ShapeDtypeStruct(val.shape[:-1] + (depth,), val.dtype)
    rows = jax.ShapeDtypeStruct((count, examples), jnp.float32)
    grams = jax.ShapeDtypeStruct((layers, 2, examples * tokens, count * tokens), jnp.float32)

    parts = [val[..., :depth], *call(cut_kernel, [part] * (cuts - 1), [VMEM], [val])]
    last = permuted(parts[-1], "blk", lambda i: i + (1, -1, 1, 3)[i % 4])
    second = [permuted(x, "blk", lambda i: i + 2) for x in parts]
    picked = [call(pick_kernel, part, [VMEM] * 2, [x, y]) for x, y in zip(parts[:-1], second)]
    first = [permuted(x, "blk", lambda i: i ^ 1) for x in picked]
    far_last = permuted(last, "blk", lambda i: i ^ 2, lambda i: i % 2 == 0)

    own = call(scores_kernel, rows, [VMEM] * 2, [train, val], work)
    far = call(scores_kernel, rows, [VMEM] * (1 + cuts), [train] + second, work)
    sums = call(grams_kernel, grams, [VMEM] * len(first), [train] + first[:-1], work // 2)
    sums = call(add_kernel, grams, [VMEM] * 5, [train, far_last, last, sums, far], work // cuts)
    out = jax.ShapeDtypeStruct((3,) + rows.shape, jnp.float32)
    kernel = functools.partial(last_kernel, depth * (cuts - 2))
    partial_rows = call(kernel, out, [VMEM] * 5, [train, first[-1], sums, own, far], work // cuts)
    return lax.psum(partial_rows, "layer").transpose(2, 0, 1)


def solution(mesh):
    return jax.shard_map(
        local,
        mesh=mesh,
        in_specs=(P("blk", "layer", None, None, None), P("blk", "layer", None, None, None)),
        out_specs=P("blk", None, None),
        check_vma=False,
    )
```

```python
import functools

import jax
import jax.numpy as jnp
from jax import lax
from jax.experimental import pallas as pl
from jax.experimental.pallas import tpu as pltpu
from jax.sharding import PartitionSpec as P

CUTS = 4
GROUP = 4

VMEM = pl.BlockSpec(memory_space=pltpu.VMEM)


def permuted(block, axis, target, sends=lambda i: True):
    size = lax.axis_size(axis)
    return lax.ppermute(block, axis, [(i, target(i) % size) for i in range(size) if sends(i)])


def call(kernel, out_shape, specs, operands, flops=0, scratch=(), vmem=16 << 20):
    shapes = list(operands) + jax.tree.leaves(out_shape)
    return pl.pallas_call(
        kernel,
        out_shape=out_shape,
        in_specs=specs,
        out_specs=jax.tree.map(lambda _: VMEM, out_shape),
        scratch_shapes=scratch,
        compiler_params=pltpu.CompilerParams(vmem_limit_bytes=vmem),
        cost_estimate=pl.CostEstimate(
            flops=flops,
            bytes_accessed=sum(x.size * x.dtype.itemsize for x in shapes),
            transcendentals=0,
        ),
    )(*operands)


def groups(train_ref):
    examples = train_ref.shape[0]
    size = GROUP if examples % GROUP == 0 else 1
    return [slice(first, first + size) for first in range(0, examples, size)]


def gram(train_ref, val_refs, layer, index, group, start=0):
    total = 0.0
    for ref in val_refs:
        depth = ref.shape[-1]
        train = train_ref[group, layer, index, :, start : start + depth].reshape(-1, depth)
        val = ref[:, layer, index].reshape(-1, depth)
        total = total + lax.dot_general(
            train, val, (((1,), (1,)), ((), ())), preferred_element_type=jnp.float32
        )
        start += depth
    return total


def token_sums(product, tokens):
    return jnp.sum(product.reshape(-1, tokens, product.shape[-1]), axis=1)


def example_sums(by_token, tokens):
    count = by_token.shape[-1] // tokens
    shape = (count, by_token.shape[-1])
    token = lax.broadcasted_iota(jnp.int32, shape, 1) // tokens
    mine = (token == lax.broadcasted_iota(jnp.int32, shape, 0)).astype(jnp.float32)
    return lax.dot_general(
        mine, by_token, (((1,), (1,)), ((), ())),
        precision=lax.Precision.HIGHEST, preferred_element_type=jnp.float32,
    )


def scores(train_ref, val_refs):
    layers, tokens = train_ref.shape[1], train_ref.shape[3]
    sums = []
    for group in groups(train_ref):
        product = 0.0
        for layer in range(layers):
            product = product + gram(train_ref, val_refs, layer, 0, group) * gram(
                train_ref, val_refs, layer, 1, group
            )
        sums.append(token_sums(product, tokens))
    return example_sums(jnp.concatenate(sums, axis=0), tokens)


def cut_kernel(val_ref, *part_refs):
    for c, ref in enumerate(part_refs):
        depth = ref.shape[-1]
        ref[...] = val_ref[..., c * depth : (c + 1) * depth]


def own_kernel(train_ref, val_ref, out_ref):
    out_ref[...] = scores(train_ref, [val_ref])


def second_kernel(train_ref, even_ref, *refs):
    *odd_refs, out_ref = refs

    def put(val_refs):
        out_ref[...] = scores(train_ref, val_refs)

    by_parity(lambda: put([even_ref]), lambda: put(odd_refs))


def by_parity(even, odd):
    parity = lax.rem(lax.axis_index("blk"), 2)
    pl.when(parity == 0)(even)
    pl.when(parity == 1)(odd)


def pick_kernel(even_ref, odd_ref, out_ref):
    def put(ref):
        out_ref[...] = ref[...]

    by_parity(lambda: put(even_ref), lambda: put(odd_ref))


def grams_kernel(train_ref, *refs):
    *part_refs, out_ref = refs
    layers, tokens = train_ref.shape[1], train_ref.shape[3]
    for layer in range(layers):
        for index in range(2):
            for group in groups(train_ref):
                rows = slice(group.start * tokens, group.stop * tokens)
                out_ref[layer, index, rows] = gram(train_ref, part_refs, layer, index, group)


def add_kernel(train_ref, even_ref, odd_ref, grams_ref, _, out_ref):
    layers, tokens, features = train_ref.shape[1], train_ref.shape[3], train_ref.shape[4]

    def add(part_ref):
        start = features - part_ref.shape[-1]
        for layer in range(layers):
            for index in range(2):
                for group in groups(train_ref):
                    rows = slice(group.start * tokens, group.stop * tokens)
                    out_ref[layer, index, rows] = grams_ref[layer, index, rows] + gram(
                        train_ref, [part_ref], layer, index, group, start
                    )

    by_parity(lambda: add(even_ref), lambda: add(odd_ref))


def last_kernel(start, train_ref, part_ref, grams_ref, own_ref, second_ref, out_ref):
    layers, tokens = train_ref.shape[1], train_ref.shape[3]
    sums = []
    for group in groups(train_ref):
        rows = slice(group.start * tokens, group.stop * tokens)
        product = 0.0
        for layer in range(layers):
            act, grad = (
                grams_ref[layer, index, rows] + gram(train_ref, [part_ref], layer, index, group, start)
                for index in range(2)
            )
            product = product + act * grad
        sums.append(token_sums(product, tokens))
    out_ref[0] = own_ref[...]
    out_ref[1] = example_sums(jnp.concatenate(sums, axis=0), tokens)
    out_ref[2] = second_ref[...]


def local(train, val):
    examples, layers, _, tokens, features = train.shape
    count = val.shape[0]
    cuts = CUTS
    depth = features // cuts
    work = 4 * examples * count * layers * tokens * tokens * features
    part = jax.ShapeDtypeStruct(val.shape[:-1] + (depth,), val.dtype)
    rows = jax.ShapeDtypeStruct((count, examples), jnp.float32)
    grams = jax.ShapeDtypeStruct((layers, 2, examples * tokens, count * tokens), jnp.float32)

    def even(i):
        return i % 2 == 0

    def odd(i):
        return i % 2 == 1

    even_block = permuted(val, "blk", lambda i: i + 2, even)
    parts = call(cut_kernel, [part] * cuts, [VMEM], [val])
    odd_parts = [permuted(x, "blk", lambda i: i + 2, odd) for x in parts]
    last = permuted(parts[-1], "blk", lambda i: i ^ 1)
    picked = [call(pick_kernel, part, [VMEM] * 2, [x, y]) for x, y in zip(parts[:-1], odd_parts)]
    first = [permuted(x, "blk", lambda i: i ^ 1) for x in picked]
    far_last = permuted(last, "blk", lambda i: i + 2, even)

    own = call(own_kernel, rows, [VMEM] * 2, [train, val], work)
    far = call(second_kernel, rows, [VMEM] * (2 + cuts), [train, even_block, *odd_parts], work)
    sums = call(grams_kernel, grams, [VMEM] * len(first), [train] + first[:-1], work // 2)
    sums = call(add_kernel, grams, [VMEM] * 5, [train, far_last, last, sums, far], work // cuts)
    out = jax.ShapeDtypeStruct((3,) + rows.shape, jnp.float32)
    kernel = functools.partial(last_kernel, depth * (cuts - 2))
    partial_rows = call(kernel, out, [VMEM] * 5, [train, first[-1], sums, own, far], work // cuts)
    return lax.psum(partial_rows, "layer").transpose(2, 0, 1)


def solution(mesh):
    return jax.shard_map(
        local,
        mesh=mesh,
        in_specs=(P("blk", "layer", None, None, None), P("blk", "layer", None, None, None)),
        out_specs=P("blk", None, None),
        check_vma=False,
    )
```

```python
import functools

import jax
import jax.numpy as jnp
from jax import lax
from jax.experimental import pallas as pl
from jax.experimental.pallas import tpu as pltpu
from jax.sharding import PartitionSpec as P

CUTS = 4
GROUP = 4

VMEM = pl.BlockSpec(memory_space=pltpu.VMEM)


def permuted(block, axis, target):
    size = lax.axis_size(axis)
    return lax.ppermute(block, axis, [(i, target(i) % size) for i in range(size)])


def call(kernel, out_shape, specs, operands, flops=0, scratch=(), vmem=16 << 20):
    shapes = list(operands) + jax.tree.leaves(out_shape)
    return pl.pallas_call(
        kernel,
        out_shape=out_shape,
        in_specs=specs,
        out_specs=jax.tree.map(lambda _: VMEM, out_shape),
        scratch_shapes=scratch,
        compiler_params=pltpu.CompilerParams(vmem_limit_bytes=vmem),
        cost_estimate=pl.CostEstimate(
            flops=flops,
            bytes_accessed=sum(x.size * x.dtype.itemsize for x in shapes),
            transcendentals=0,
        ),
    )(*operands)


def groups(train_ref):
    examples = train_ref.shape[0]
    size = GROUP if examples % GROUP == 0 else 1
    return [slice(first, first + size) for first in range(0, examples, size)]


def gram(train_ref, val_refs, layer, index, group, start=0):
    total = 0.0
    for ref in val_refs:
        depth = ref.shape[-1]
        train = train_ref[group, layer, index, :, start : start + depth].reshape(-1, depth)
        val = ref[:, layer, index].reshape(-1, depth)
        total = total + lax.dot_general(
            train, val, (((1,), (1,)), ((), ())), preferred_element_type=jnp.float32
        )
        start += depth
    return total


def token_sums(product, tokens):
    return jnp.sum(product.reshape(-1, tokens, product.shape[-1]), axis=1)


def example_sums(by_token, tokens):
    count = by_token.shape[-1] // tokens
    shape = (count, by_token.shape[-1])
    token = lax.broadcasted_iota(jnp.int32, shape, 1) // tokens
    mine = (token == lax.broadcasted_iota(jnp.int32, shape, 0)).astype(jnp.float32)
    return lax.dot_general(
        mine, by_token, (((1,), (1,)), ((), ())),
        precision=lax.Precision.HIGHEST, preferred_element_type=jnp.float32,
    )


def scores(train_ref, val_refs):
    layers, tokens = train_ref.shape[1], train_ref.shape[3]
    sums = []
    for group in groups(train_ref):
        product = 0.0
        for layer in range(layers):
            product = product + gram(train_ref, val_refs, layer, 0, group) * gram(
                train_ref, val_refs, layer, 1, group
            )
        sums.append(token_sums(product, tokens))
    return example_sums(jnp.concatenate(sums, axis=0), tokens)


def cut_kernel(val_ref, *part_refs):
    for c, ref in enumerate(part_refs, 1):
        depth = ref.shape[-1]
        ref[...] = val_ref[..., c * depth : (c + 1) * depth]


def scores_kernel(train_ref, *refs):
    *val_refs, out_ref = refs
    out_ref[...] = scores(train_ref, val_refs)


def by_parity(even, odd):
    parity = lax.rem(lax.axis_index("blk"), 2)
    pl.when(parity == 0)(even)
    pl.when(parity == 1)(odd)


def pick_kernel(even_ref, odd_ref, *refs):
    out_ref = refs[-1]

    def put(ref):
        out_ref[...] = ref[...]

    by_parity(lambda: put(even_ref), lambda: put(odd_ref))


def pick_last_kernel(even_ref, odd_ref, out_ref):
    count = out_ref.shape[0]

    def put(ref):
        out_ref[...] = ref[ref.shape[0] - count :]

    by_parity(lambda: put(even_ref), lambda: put(odd_ref))


def columns(first, count, tokens):
    return slice(first * tokens, (first + count) * tokens)


def grams_kernel(train_ref, *refs):
    *part_refs, out_ref = refs
    layers, tokens = train_ref.shape[1], train_ref.shape[3]
    for layer in range(layers):
        for index in range(2):
            for group in groups(train_ref):
                rows = slice(group.start * tokens, group.stop * tokens)
                out_ref[layer, index, rows] = gram(train_ref, part_refs, layer, index, group)


def add_kernel(start, train_ref, far_ref, near_ref, part_ref, grams_ref, out_ref):
    layers, tokens, features = train_ref.shape[1], train_ref.shape[3], train_ref.shape[4]
    detour = columns(0, far_ref.shape[0], tokens)
    rest = slice(detour.stop, grams_ref.shape[-1])

    def add(last_ref):
        begin = features - last_ref.shape[-1]
        for layer in range(layers):
            for index in range(2):
                for group in groups(train_ref):
                    rows = slice(group.start * tokens, group.stop * tokens)
                    total = grams_ref[layer, index, rows] + gram(
                        train_ref, [part_ref], layer, index, group, start
                    )
                    out_ref[layer, index, rows, detour] = total[:, detour] + gram(
                        train_ref, [last_ref], layer, index, group, begin
                    )
                    out_ref[layer, index, rows, rest] = total[:, rest]

    by_parity(lambda: add(far_ref), lambda: add(near_ref))


def last_kernel(train_ref, part_ref, grams_ref, own_ref, second_ref, out_ref):
    layers, tokens, features = train_ref.shape[1], train_ref.shape[3], train_ref.shape[4]
    begin = features - part_ref.shape[-1]
    total_columns = grams_ref.shape[-1]
    rest = slice(total_columns - part_ref.shape[0] * tokens, total_columns)
    detour = slice(0, rest.start)
    sums = []
    for group in groups(train_ref):
        rows = slice(group.start * tokens, group.stop * tokens)
        products = [0.0, 0.0]
        for layer in range(layers):
            act, grad = (
                grams_ref[layer, index, rows, rest]
                + gram(train_ref, [part_ref], layer, index, group, begin)
                for index in range(2)
            )
            products[1] = products[1] + act * grad
            products[0] = products[0] + (
                grams_ref[layer, 0, rows, detour] * grams_ref[layer, 1, rows, detour]
            )
        sums.append([token_sums(x, tokens) for x in products])
    out_ref[0] = own_ref[...]
    out_ref[1] = jnp.concatenate(
        [example_sums(jnp.concatenate(x, axis=0), tokens) for x in zip(*sums)], axis=0
    )
    out_ref[2] = second_ref[...]


def local(train, val):
    examples, layers, _, tokens, features = train.shape
    count = val.shape[0]
    cuts = CUTS
    depth = features // cuts
    work = 4 * examples * count * layers * tokens * tokens * features
    part = jax.ShapeDtypeStruct(val.shape[:-1] + (depth,), val.dtype)
    small = jax.ShapeDtypeStruct((1,) + part.shape[1:], val.dtype)
    rows = jax.ShapeDtypeStruct((count, examples), jnp.float32)
    grams = jax.ShapeDtypeStruct((layers, 2, examples * tokens, count * tokens), jnp.float32)

    detour = val[: count - 1, ..., (cuts - 1) * depth :]
    parts = [val[..., :depth], *call(cut_kernel, [part] * (cuts - 1), [VMEM], [val])]
    second = [permuted(x, "blk", lambda i: i + 2) for x in parts]
    near_last = permuted(detour, "blk", lambda i: i ^ 1)
    far_last = permuted(near_last, "blk", lambda i: i + 2)
    first = []
    for c in range(cuts - 1):
        operands = [parts[c], second[c]] + ([near_last] if c == 1 else [])
        picked = call(pick_kernel, part, [VMEM] * len(operands), operands)
        first.append(permuted(picked, "blk", lambda i: i ^ 1))
    picked = call(pick_last_kernel, small, [VMEM] * 2, [parts[-1], second[-1]])
    end = permuted(picked, "blk", lambda i: i ^ 1)

    own = call(scores_kernel, rows, [VMEM] * 2, [train, val], work)
    far = call(scores_kernel, rows, [VMEM] * (1 + cuts), [train] + second, work)
    sums = call(grams_kernel, grams, [VMEM] * (cuts - 1), [train] + first[:-1], work // 2)
    operands = [train, far_last, near_last, first[-1], sums]
    kernel = functools.partial(add_kernel, depth * (cuts - 2))
    sums = call(kernel, grams, [VMEM] * len(operands), operands, work // 2)
    out = jax.ShapeDtypeStruct((3,) + rows.shape, jnp.float32)
    partial_rows = call(last_kernel, out, [VMEM] * 5, [train, end, sums, own, far], work // cuts)
    return lax.psum(partial_rows, "layer").transpose(2, 0, 1)


def solution(mesh):
    return jax.shard_map(
        local,
        mesh=mesh,
        in_specs=(P("blk", "layer", None, None, None), P("blk", "layer", None, None, None)),
        out_specs=P("blk", None, None),
        check_vma=False,
    )
```

```python
import functools

import jax
import jax.numpy as jnp
from jax import lax
from jax.experimental import pallas as pl
from jax.experimental.pallas import tpu as pltpu
from jax.sharding import PartitionSpec as P

CUTS = 4
GROUP = 4

VMEM = pl.BlockSpec(memory_space=pltpu.VMEM)


def permuted(block, axis, target):
    size = lax.axis_size(axis)
    return lax.ppermute(block, axis, [(i, target(i) % size) for i in range(size)])


def call(kernel, out_shape, specs, operands, flops=0, scratch=(), vmem=16 << 20):
    shapes = list(operands) + jax.tree.leaves(out_shape)
    return pl.pallas_call(
        kernel,
        out_shape=out_shape,
        in_specs=specs,
        out_specs=jax.tree.map(lambda _: VMEM, out_shape),
        scratch_shapes=scratch,
        compiler_params=pltpu.CompilerParams(vmem_limit_bytes=vmem),
        cost_estimate=pl.CostEstimate(
            flops=flops,
            bytes_accessed=sum(x.size * x.dtype.itemsize for x in shapes),
            transcendentals=0,
        ),
    )(*operands)


def groups(train_ref):
    examples = train_ref.shape[0]
    size = GROUP if examples % GROUP == 0 else 1
    return [slice(first, first + size) for first in range(0, examples, size)]


def gram(train_ref, val_refs, layer, index, group, start=0):
    total = 0.0
    for ref in val_refs:
        depth = ref.shape[-1]
        train = train_ref[group, layer, index, :, start : start + depth].reshape(-1, depth)
        val = ref[:, layer, index].reshape(-1, depth)
        total = total + lax.dot_general(
            train, val, (((1,), (1,)), ((), ())), preferred_element_type=jnp.float32
        )
        start += depth
    return total


def token_sums(product, tokens):
    return jnp.sum(product.reshape(-1, tokens, product.shape[-1]), axis=1)


def example_sums(by_token, tokens):
    count = by_token.shape[-1] // tokens
    shape = (count, by_token.shape[-1])
    token = lax.broadcasted_iota(jnp.int32, shape, 1) // tokens
    mine = (token == lax.broadcasted_iota(jnp.int32, shape, 0)).astype(jnp.float32)
    return lax.dot_general(
        mine, by_token, (((1,), (1,)), ((), ())),
        precision=lax.Precision.HIGHEST, preferred_element_type=jnp.float32,
    )


def scores(train_ref, val_refs):
    layers, tokens = train_ref.shape[1], train_ref.shape[3]
    sums = []
    for group in groups(train_ref):
        product = 0.0
        for layer in range(layers):
            product = product + gram(train_ref, val_refs, layer, 0, group) * gram(
                train_ref, val_refs, layer, 1, group
            )
        sums.append(token_sums(product, tokens))
    return example_sums(jnp.concatenate(sums, axis=0), tokens)


def cut_kernel(val_ref, *part_refs):
    for c, ref in enumerate(part_refs, 1):
        depth = ref.shape[-1]
        ref[...] = val_ref[..., c * depth : (c + 1) * depth]


def scores_kernel(train_ref, *refs):
    *val_refs, out_ref = refs
    out_ref[...] = scores(train_ref, val_refs)


def by_parity(even, odd):
    parity = lax.rem(lax.axis_index("blk"), 2)
    pl.when(parity == 0)(even)
    pl.when(parity == 1)(odd)


def pick_kernel(even_ref, odd_ref, *refs):
    out_ref = refs[-1]

    def put(ref):
        out_ref[...] = ref[...]

    by_parity(lambda: put(even_ref), lambda: put(odd_ref))


def pick_last_kernel(even_ref, odd_ref, out_ref):
    count = out_ref.shape[0]

    def put(ref):
        out_ref[...] = ref[ref.shape[0] - count :]

    by_parity(lambda: put(even_ref), lambda: put(odd_ref))


def columns(first, count, tokens):
    return slice(first * tokens, (first + count) * tokens)


def grams_kernel(train_ref, *refs):
    *part_refs, out_ref = refs
    layers, tokens = train_ref.shape[1], train_ref.shape[3]
    for layer in range(layers):
        for index in range(2):
            for group in groups(train_ref):
                rows = slice(group.start * tokens, group.stop * tokens)
                out_ref[layer, index, rows] = gram(train_ref, part_refs, layer, index, group)


def add_kernel(train_ref, far_ref, near_ref, grams_ref, out_ref):
    layers, tokens, features = train_ref.shape[1], train_ref.shape[3], train_ref.shape[4]
    detour = columns(0, far_ref.shape[0], tokens)
    rest = slice(detour.stop, grams_ref.shape[-1])

    def add(last_ref):
        begin = features - last_ref.shape[-1]
        for layer in range(layers):
            for index in range(2):
                for group in groups(train_ref):
                    rows = slice(group.start * tokens, group.stop * tokens)
                    out_ref[layer, index, rows, detour] = grams_ref[layer, index, rows, detour] + gram(
                        train_ref, [last_ref], layer, index, group, begin
                    )

    out_ref[..., rest] = grams_ref[..., rest]
    by_parity(lambda: add(far_ref), lambda: add(near_ref))


def last_kernel(train_ref, part_ref, end_ref, grams_ref, own_ref, second_ref, out_ref):
    layers, tokens, features = train_ref.shape[1], train_ref.shape[3], train_ref.shape[4]
    depth, total_columns = part_ref.shape[-1], grams_ref.shape[-1]
    rest = slice(total_columns - end_ref.shape[0] * tokens, total_columns)
    detour = slice(0, rest.start)
    sums = []
    for group in groups(train_ref):
        rows = slice(group.start * tokens, group.stop * tokens)
        products = [0.0, 0.0]
        for layer in range(layers):
            totals = []
            for index in range(2):
                total = grams_ref[layer, index, rows] + gram(
                    train_ref, [part_ref], layer, index, group, features - 2 * depth
                )
                end = gram(train_ref, [end_ref], layer, index, group, features - depth)
                totals.append((total[:, detour], total[:, rest] + end))
            products = [x + act * grad for x, act, grad in zip(products, *totals)]
        sums.append([token_sums(x, tokens) for x in products])
    out_ref[0] = own_ref[...]
    out_ref[1] = jnp.concatenate(
        [example_sums(jnp.concatenate(x, axis=0), tokens) for x in zip(*sums)], axis=0
    )
    out_ref[2] = second_ref[...]


def summed(rows, axis):
    if lax.axis_size(axis) != 2:
        return lax.psum(rows, axis)
    return rows + permuted(rows, axis, lambda i: i ^ 1)


def local(train, val):
    examples, layers, _, tokens, features = train.shape
    count = val.shape[0]
    cuts = CUTS
    depth = features // cuts
    work = 4 * examples * count * layers * tokens * tokens * features
    part = jax.ShapeDtypeStruct(val.shape[:-1] + (depth,), val.dtype)
    small = jax.ShapeDtypeStruct((1,) + part.shape[1:], val.dtype)
    rows = jax.ShapeDtypeStruct((count, examples), jnp.float32)
    grams = jax.ShapeDtypeStruct((layers, 2, examples * tokens, count * tokens), jnp.float32)

    detour = val[: count - 1, ..., (cuts - 1) * depth :]
    parts = [val[..., :depth], *call(cut_kernel, [part] * (cuts - 1), [VMEM], [val])]
    second = [permuted(x, "blk", lambda i: i + 2) for x in parts]
    near_last = permuted(detour, "blk", lambda i: i ^ 1)
    far_last = permuted(near_last, "blk", lambda i: i + 2)
    first = []
    for c in range(cuts - 1):
        operands = [parts[c], second[c]] + ([near_last] if c == 1 else [])
        picked = call(pick_kernel, part, [VMEM] * len(operands), operands)
        first.append(permuted(picked, "blk", lambda i: i ^ 1))
    picked = call(pick_last_kernel, small, [VMEM] * 2, [parts[-1], second[-1]])
    end = permuted(picked, "blk", lambda i: i ^ 1)

    own = call(scores_kernel, rows, [VMEM] * 2, [train, val], work)
    far = call(scores_kernel, rows, [VMEM] * (1 + cuts), [train] + second, work)
    sums = call(grams_kernel, grams, [VMEM] * (cuts - 1), [train] + first[:-1], work // 2)
    sums = call(add_kernel, grams, [VMEM] * 4, [train, far_last, near_last, sums], work // cuts)
    out = jax.ShapeDtypeStruct((3,) + rows.shape, jnp.float32)
    operands = [train, first[-1], end, sums, own, far]
    partial_rows = call(last_kernel, out, [VMEM] * len(operands), operands, work // 2)
    return summed(partial_rows, "layer").transpose(2, 0, 1)


def solution(mesh):
    return jax.shard_map(
        local,
        mesh=mesh,
        in_specs=(P("blk", "layer", None, None, None), P("blk", "layer", None, None, None)),
        out_specs=P("blk", None, None),
        check_vma=False,
    )
```

```python
import functools

import jax
import jax.numpy as jnp
from jax import lax
from jax.experimental import pallas as pl
from jax.experimental.pallas import tpu as pltpu
from jax.sharding import PartitionSpec as P

CUTS = 4
GROUP = 4

VMEM = pl.BlockSpec(memory_space=pltpu.VMEM)


def permuted(block, axis, target):
    size = lax.axis_size(axis)
    return lax.ppermute(block, axis, [(i, target(i) % size) for i in range(size)])


def call(kernel, out_shape, specs, operands, flops=0, scratch=(), vmem=16 << 20):
    shapes = list(operands) + jax.tree.leaves(out_shape)
    return pl.pallas_call(
        kernel,
        out_shape=out_shape,
        in_specs=specs,
        out_specs=jax.tree.map(lambda _: VMEM, out_shape),
        scratch_shapes=scratch,
        compiler_params=pltpu.CompilerParams(vmem_limit_bytes=vmem),
        cost_estimate=pl.CostEstimate(
            flops=flops,
            bytes_accessed=sum(x.size * x.dtype.itemsize for x in shapes),
            transcendentals=0,
        ),
    )(*operands)


def groups(train_ref):
    examples = train_ref.shape[0]
    size = GROUP if examples % GROUP == 0 else 1
    return [slice(first, first + size) for first in range(0, examples, size)]


def gram(train_ref, val_refs, layer, index, group, start=0):
    total = 0.0
    for ref in val_refs:
        depth = ref.shape[-1]
        train = train_ref[group, layer, index, :, start : start + depth].reshape(-1, depth)
        val = ref[:, layer, index].reshape(-1, depth)
        total = total + lax.dot_general(
            train, val, (((1,), (1,)), ((), ())), preferred_element_type=jnp.float32
        )
        start += depth
    return total


def token_sums(product, tokens):
    return jnp.sum(product.reshape(-1, tokens, product.shape[-1]), axis=1)


def example_sums(by_token, tokens):
    count = by_token.shape[-1] // tokens
    shape = (count, by_token.shape[-1])
    token = lax.broadcasted_iota(jnp.int32, shape, 1) // tokens
    mine = (token == lax.broadcasted_iota(jnp.int32, shape, 0)).astype(jnp.float32)
    return lax.dot_general(
        mine, by_token, (((1,), (1,)), ((), ())),
        precision=lax.Precision.HIGHEST, preferred_element_type=jnp.float32,
    )


def scores(train_ref, val_refs):
    layers, tokens = train_ref.shape[1], train_ref.shape[3]
    sums = []
    for group in groups(train_ref):
        product = 0.0
        for layer in range(layers):
            product = product + gram(train_ref, val_refs, layer, 0, group) * gram(
                train_ref, val_refs, layer, 1, group
            )
        sums.append(token_sums(product, tokens))
    return example_sums(jnp.concatenate(sums, axis=0), tokens)


def cut_kernel(val_ref, *part_refs):
    for c, ref in enumerate(part_refs, 1):
        depth = ref.shape[-1]
        ref[...] = val_ref[..., c * depth : (c + 1) * depth]


def scores_kernel(train_ref, *refs):
    *val_refs, out_ref = refs
    out_ref[...] = scores(train_ref, val_refs)


def by_parity(even, odd):
    parity = lax.rem(lax.axis_index("blk"), 2)
    pl.when(parity == 0)(even)
    pl.when(parity == 1)(odd)


def pick_kernel(even_ref, odd_ref, *refs):
    out_ref = refs[-1]

    def put(ref):
        out_ref[...] = ref[...]

    by_parity(lambda: put(even_ref), lambda: put(odd_ref))


def pick_last_kernel(even_ref, odd_ref, out_ref):
    count = out_ref.shape[0]

    def put(ref):
        out_ref[...] = ref[ref.shape[0] - count :]

    by_parity(lambda: put(even_ref), lambda: put(odd_ref))


def columns(first, count, tokens):
    return slice(first * tokens, (first + count) * tokens)


def grams_kernel(train_ref, *refs):
    *part_refs, out_ref = refs
    layers, tokens = train_ref.shape[1], train_ref.shape[3]
    for layer in range(layers):
        for index in range(2):
            for group in groups(train_ref):
                rows = slice(group.start * tokens, group.stop * tokens)
                out_ref[layer, index, rows] = gram(train_ref, part_refs, layer, index, group)


def add_kernel(train_ref, far_ref, near_ref, grams_ref, out_ref):
    layers, tokens, features = train_ref.shape[1], train_ref.shape[3], train_ref.shape[4]
    detour = columns(0, far_ref.shape[0], tokens)
    rest = slice(detour.stop, grams_ref.shape[-1])

    def add(last_ref):
        begin = features - last_ref.shape[-1]
        for layer in range(layers):
            for index in range(2):
                for group in groups(train_ref):
                    rows = slice(group.start * tokens, group.stop * tokens)
                    out_ref[layer, index, rows, detour] = grams_ref[layer, index, rows, detour] + gram(
                        train_ref, [last_ref], layer, index, group, begin
                    )

    out_ref[..., rest] = grams_ref[..., rest]
    by_parity(lambda: add(far_ref), lambda: add(near_ref))


def last_kernel(train_ref, part_ref, end_ref, grams_ref, own_ref, second_ref, out_ref):
    layers, tokens, features = train_ref.shape[1], train_ref.shape[3], train_ref.shape[4]
    depth, total_columns = part_ref.shape[-1], grams_ref.shape[-1]
    rest = slice(total_columns - end_ref.shape[0] * tokens, total_columns)
    detour = slice(0, rest.start)
    sums = []
    for group in groups(train_ref):
        rows = slice(group.start * tokens, group.stop * tokens)
        products = [0.0, 0.0]
        for layer in range(layers):
            totals = []
            for index in range(2):
                total = grams_ref[layer, index, rows] + gram(
                    train_ref, [part_ref], layer, index, group, features - 2 * depth
                )
                end = gram(train_ref, [end_ref], layer, index, group, features - depth)
                totals.append((total[:, detour], total[:, rest] + end))
            products = [x + act * grad for x, act, grad in zip(products, *totals)]
        sums.append([token_sums(x, tokens) for x in products])
    out_ref[0] = own_ref[...]
    out_ref[1] = jnp.concatenate(
        [example_sums(jnp.concatenate(x, axis=0), tokens) for x in zip(*sums)], axis=0
    )
    out_ref[2] = second_ref[...]


def summed(rows, axis):
    if lax.axis_size(axis) != 2:
        return lax.psum(rows, axis)
    return rows + permuted(rows, axis, lambda i: i ^ 1)


def local(train, val):
    examples, layers, _, tokens, features = train.shape
    count = val.shape[0]
    cuts = CUTS
    depth = features // cuts
    work = 4 * examples * count * layers * tokens * tokens * features
    part = jax.ShapeDtypeStruct(val.shape[:-1] + (depth,), val.dtype)
    small = jax.ShapeDtypeStruct((1,) + part.shape[1:], val.dtype)
    rows = jax.ShapeDtypeStruct((count, examples), jnp.float32)
    grams = jax.ShapeDtypeStruct((layers, 2, examples * tokens, count * tokens), jnp.float32)

    detour = val[: count - 1, ..., (cuts - 1) * depth :]
    parts = [val[..., :depth], *call(cut_kernel, [part] * (cuts - 1), [VMEM], [val])]
    second = [permuted(x, "blk", lambda i: i + 2) for x in parts]
    near_last = permuted(detour, "blk", lambda i: i ^ 1)
    far_last = permuted(near_last, "blk", lambda i: i + 2)
    first = []
    for c in range(cuts - 1):
        operands = [parts[c], second[c]] + ([near_last] if c == 1 else [])
        picked = call(pick_kernel, part, [VMEM] * len(operands), operands)
        first.append(permuted(picked, "blk", lambda i: i ^ 1))
    picked = call(pick_last_kernel, small, [VMEM] * 2, [parts[-1], second[-1]])
    end = permuted(picked, "blk", lambda i: i ^ 1)

    own = call(scores_kernel, rows, [VMEM] * 2, [train, val], work)
    far = call(scores_kernel, rows, [VMEM] * (1 + cuts), [train] + second, work)
    sums = call(grams_kernel, grams, [VMEM] * (cuts - 1), [train] + first[:-1], work // 2)
    sums = call(add_kernel, grams, [VMEM] * 4, [train, far_last, near_last, sums], 2 * work)
    out = jax.ShapeDtypeStruct((3,) + rows.shape, jnp.float32)
    operands = [train, first[-1], end, sums, own, far]
    partial_rows = call(last_kernel, out, [VMEM] * len(operands), operands, work // 2)
    return summed(partial_rows, "layer").transpose(2, 0, 1)


def solution(mesh):
    return jax.shard_map(
        local,
        mesh=mesh,
        in_specs=(P("blk", "layer", None, None, None), P("blk", "layer", None, None, None)),
        out_specs=P("blk", None, None),
        check_vma=False,
    )
```

```python
import functools

import jax
import jax.numpy as jnp
from jax import lax
from jax.experimental import pallas as pl
from jax.experimental.pallas import tpu as pltpu
from jax.sharding import PartitionSpec as P

CUTS = 4
GROUP = 4

VMEM = pl.BlockSpec(memory_space=pltpu.VMEM)
HBM = pl.BlockSpec(memory_space=pltpu.HBM)


def permuted(block, axis, target):
    size = lax.axis_size(axis)
    return lax.ppermute(block, axis, [(i, target(i) % size) for i in range(size)])


def call(kernel, out_shape, specs, operands, flops=0, scratch=(), vmem=16 << 20):
    shapes = list(operands) + jax.tree.leaves(out_shape)
    return pl.pallas_call(
        kernel,
        out_shape=out_shape,
        in_specs=specs,
        out_specs=jax.tree.map(lambda _: VMEM, out_shape),
        scratch_shapes=scratch,
        compiler_params=pltpu.CompilerParams(vmem_limit_bytes=vmem),
        cost_estimate=pl.CostEstimate(
            flops=flops,
            bytes_accessed=sum(x.size * x.dtype.itemsize for x in shapes),
            transcendentals=0,
        ),
    )(*operands)


def groups(train_ref):
    examples = train_ref.shape[0]
    size = GROUP if examples % GROUP == 0 else 1
    return [slice(first, first + size) for first in range(0, examples, size)]


def gram(train_ref, val_refs, layer, index, group, start=0):
    total = 0.0
    for ref in val_refs:
        depth = ref.shape[-1]
        train = train_ref[group, layer, index, :, start : start + depth].reshape(-1, depth)
        val = ref[:, layer, index].reshape(-1, depth)
        total = total + lax.dot_general(
            train, val, (((1,), (1,)), ((), ())), preferred_element_type=jnp.float32
        )
        start += depth
    return total


def token_sums(product, tokens):
    return jnp.sum(product.reshape(-1, tokens, product.shape[-1]), axis=1)


def example_sums(by_token, tokens):
    count = by_token.shape[-1] // tokens
    shape = (count, by_token.shape[-1])
    token = lax.broadcasted_iota(jnp.int32, shape, 1) // tokens
    mine = (token == lax.broadcasted_iota(jnp.int32, shape, 0)).astype(jnp.float32)
    return lax.dot_general(
        mine, by_token, (((1,), (1,)), ((), ())),
        precision=lax.Precision.HIGHEST, preferred_element_type=jnp.float32,
    )


def scores(train_ref, val_refs):
    layers, tokens = train_ref.shape[1], train_ref.shape[3]
    sums = []
    for group in groups(train_ref):
        product = 0.0
        for layer in range(layers):
            product = product + gram(train_ref, val_refs, layer, 0, group) * gram(
                train_ref, val_refs, layer, 1, group
            )
        sums.append(token_sums(product, tokens))
    return example_sums(jnp.concatenate(sums, axis=0), tokens)


def cut_kernel(val_ref, detour_ref, *refs):
    *part_refs, sems = refs
    depth = part_refs[0].shape[-1]
    copies = [
        pltpu.make_async_copy(val_ref.at[..., c * depth : (c + 1) * depth], ref, sems.at[c])
        for c, ref in enumerate(part_refs)
    ]
    last = val_ref.at[: detour_ref.shape[0], ..., (len(part_refs) - 1) * depth :]
    copies.append(pltpu.make_async_copy(last, detour_ref, sems.at[len(part_refs)]))
    for copy in copies:
        copy.start()
    for copy in copies:
        copy.wait()


def scores_kernel(train_ref, *refs):
    *val_refs, out_ref = refs
    out_ref[...] = scores(train_ref, val_refs)


def by_parity(even, odd):
    parity = lax.rem(lax.axis_index("blk"), 2)
    pl.when(parity == 0)(even)
    pl.when(parity == 1)(odd)


def pick_kernel(even_ref, odd_ref, *refs):
    out_ref = refs[-1]

    def put(ref):
        out_ref[...] = ref[...]

    by_parity(lambda: put(even_ref), lambda: put(odd_ref))


def pick_last_kernel(even_ref, odd_ref, out_ref):
    count = out_ref.shape[0]

    def put(ref):
        out_ref[...] = ref[ref.shape[0] - count :]

    by_parity(lambda: put(even_ref), lambda: put(odd_ref))


def columns(first, count, tokens):
    return slice(first * tokens, (first + count) * tokens)


def grams_kernel(train_ref, *refs):
    *part_refs, out_ref = refs
    layers, tokens = train_ref.shape[1], train_ref.shape[3]
    for layer in range(layers):
        for index in range(2):
            for group in groups(train_ref):
                rows = slice(group.start * tokens, group.stop * tokens)
                out_ref[layer, index, rows] = gram(train_ref, part_refs, layer, index, group)


def add_kernel(train_ref, far_ref, near_ref, grams_ref, out_ref):
    layers, tokens, features = train_ref.shape[1], train_ref.shape[3], train_ref.shape[4]
    detour = columns(0, far_ref.shape[0], tokens)
    rest = slice(detour.stop, grams_ref.shape[-1])

    def add(last_ref):
        begin = features - last_ref.shape[-1]
        for layer in range(layers):
            for index in range(2):
                for group in groups(train_ref):
                    rows = slice(group.start * tokens, group.stop * tokens)
                    out_ref[layer, index, rows, detour] = grams_ref[layer, index, rows, detour] + gram(
                        train_ref, [last_ref], layer, index, group, begin
                    )

    out_ref[..., rest] = grams_ref[..., rest]
    by_parity(lambda: add(far_ref), lambda: add(near_ref))


def last_kernel(train_ref, part_ref, end_ref, grams_ref, own_ref, second_ref, out_ref):
    layers, tokens, features = train_ref.shape[1], train_ref.shape[3], train_ref.shape[4]
    depth, total_columns = part_ref.shape[-1], grams_ref.shape[-1]
    rest = slice(total_columns - end_ref.shape[0] * tokens, total_columns)
    detour = slice(0, rest.start)
    sums = []
    for group in groups(train_ref):
        rows = slice(group.start * tokens, group.stop * tokens)
        products = [0.0, 0.0]
        for layer in range(layers):
            totals = []
            for index in range(2):
                total = grams_ref[layer, index, rows] + gram(
                    train_ref, [part_ref], layer, index, group, features - 2 * depth
                )
                end = gram(train_ref, [end_ref], layer, index, group, features - depth)
                totals.append((total[:, detour], total[:, rest] + end))
            products = [x + act * grad for x, act, grad in zip(products, *totals)]
        sums.append([token_sums(x, tokens) for x in products])
    out_ref[0] = own_ref[...]
    out_ref[1] = jnp.concatenate(
        [example_sums(jnp.concatenate(x, axis=0), tokens) for x in zip(*sums)], axis=0
    )
    out_ref[2] = second_ref[...]


def summed(rows, axis):
    if lax.axis_size(axis) != 2:
        return lax.psum(rows, axis)
    return rows + permuted(rows, axis, lambda i: i ^ 1)


def local(train, val):
    examples, layers, _, tokens, features = train.shape
    count = val.shape[0]
    cuts = CUTS
    depth = features // cuts
    work = 4 * examples * count * layers * tokens * tokens * features
    part = jax.ShapeDtypeStruct(val.shape[:-1] + (depth,), val.dtype)
    small = jax.ShapeDtypeStruct((1,) + part.shape[1:], val.dtype)
    rows = jax.ShapeDtypeStruct((count, examples), jnp.float32)
    grams = jax.ShapeDtypeStruct((layers, 2, examples * tokens, count * tokens), jnp.float32)

    detour = jax.ShapeDtypeStruct((count - 1,) + part.shape[1:], val.dtype)
    detour, *parts = call(
        cut_kernel,
        [detour] + [part] * cuts,
        [HBM],
        [val],
        scratch=[pltpu.SemaphoreType.DMA((cuts + 1,))],
        vmem=52 << 20,
    )
    second = [permuted(x, "blk", lambda i: i + 2) for x in parts]
    near_last = permuted(detour, "blk", lambda i: i ^ 1)
    far_last = permuted(near_last, "blk", lambda i: i + 2)
    first = []
    for c in range(cuts - 1):
        operands = [parts[c], second[c]] + ([near_last] if c == 1 else [])
        picked = call(pick_kernel, part, [VMEM] * len(operands), operands)
        first.append(permuted(picked, "blk", lambda i: i ^ 1))
    picked = call(pick_last_kernel, small, [VMEM] * 2, [parts[-1], second[-1]])
    end = permuted(picked, "blk", lambda i: i ^ 1)

    own = call(scores_kernel, rows, [VMEM] * 2, [train, val], work)
    far = call(scores_kernel, rows, [VMEM] * (1 + cuts), [train] + second, work)
    sums = call(grams_kernel, grams, [VMEM] * (cuts - 1), [train] + first[:-1], work // 2)
    sums = call(add_kernel, grams, [VMEM] * 4, [train, far_last, near_last, sums], 2 * work)
    out = jax.ShapeDtypeStruct((3,) + rows.shape, jnp.float32)
    operands = [train, first[-1], end, sums, own, far]
    partial_rows = call(last_kernel, out, [VMEM] * len(operands), operands, work // 2)
    return summed(partial_rows, "layer").transpose(2, 0, 1)


def solution(mesh):
    return jax.shard_map(
        local,
        mesh=mesh,
        in_specs=(P("blk", "layer", None, None, None), P("blk", "layer", None, None, None)),
        out_specs=P("blk", None, None),
        check_vma=False,
    )
```

```python
import functools

import jax
import jax.numpy as jnp
from jax import lax
from jax.experimental import pallas as pl
from jax.experimental.pallas import tpu as pltpu
from jax.sharding import PartitionSpec as P

CUTS = 4
GROUP = 4

VMEM = pl.BlockSpec(memory_space=pltpu.VMEM)


def permuted(block, axis, target):
    size = lax.axis_size(axis)
    return lax.ppermute(block, axis, [(i, target(i) % size) for i in range(size)])


def call(kernel, out_shape, specs, operands, flops=0, scratch=(), vmem=16 << 20):
    shapes = list(operands) + jax.tree.leaves(out_shape)
    return pl.pallas_call(
        kernel,
        out_shape=out_shape,
        in_specs=specs,
        out_specs=jax.tree.map(lambda _: VMEM, out_shape),
        scratch_shapes=scratch,
        compiler_params=pltpu.CompilerParams(vmem_limit_bytes=vmem),
        cost_estimate=pl.CostEstimate(
            flops=flops,
            bytes_accessed=sum(x.size * x.dtype.itemsize for x in shapes),
            transcendentals=0,
        ),
    )(*operands)


def groups(train_ref):
    examples = train_ref.shape[0]
    size = GROUP if examples % GROUP == 0 else 1
    return [slice(first, first + size) for first in range(0, examples, size)]


def gram(train_ref, val_refs, layer, index, group, start=0):
    total = 0.0
    for ref in val_refs:
        depth = ref.shape[-1]
        train = train_ref[group, layer, index, :, start : start + depth].reshape(-1, depth)
        val = ref[:, layer, index].reshape(-1, depth)
        total = total + lax.dot_general(
            train, val, (((1,), (1,)), ((), ())), preferred_element_type=jnp.float32
        )
        start += depth
    return total


def token_sums(product, tokens):
    return jnp.sum(product.reshape(-1, tokens, product.shape[-1]), axis=1)


def example_sums(by_token, tokens):
    count = by_token.shape[-1] // tokens
    shape = (count, by_token.shape[-1])
    token = lax.broadcasted_iota(jnp.int32, shape, 1) // tokens
    mine = (token == lax.broadcasted_iota(jnp.int32, shape, 0)).astype(jnp.float32)
    return lax.dot_general(
        mine, by_token, (((1,), (1,)), ((), ())),
        precision=lax.Precision.HIGHEST, preferred_element_type=jnp.float32,
    )


def scores(train_ref, val_refs):
    layers, tokens = train_ref.shape[1], train_ref.shape[3]
    sums = []
    for group in groups(train_ref):
        product = 0.0
        for layer in range(layers):
            product = product + gram(train_ref, val_refs, layer, 0, group) * gram(
                train_ref, val_refs, layer, 1, group
            )
        sums.append(token_sums(product, tokens))
    return example_sums(jnp.concatenate(sums, axis=0), tokens)


def cut_kernel(val_ref, *part_refs):
    for c, ref in enumerate(part_refs, 1):
        depth = ref.shape[-1]
        ref[...] = val_ref[..., c * depth : (c + 1) * depth]


def scores_kernel(train_ref, *refs):
    *val_refs, out_ref = refs
    out_ref[...] = scores(train_ref, val_refs)


def by_parity(even, odd):
    parity = lax.rem(lax.axis_index("blk"), 2)
    pl.when(parity == 0)(even)
    pl.when(parity == 1)(odd)


def pick_kernel(even_ref, odd_ref, *refs):
    out_ref = refs[-1]

    def put(ref):
        out_ref[...] = ref[...]

    by_parity(lambda: put(even_ref), lambda: put(odd_ref))


def pick_last_kernel(even_ref, odd_ref, out_ref):
    count = out_ref.shape[0]

    def put(ref):
        out_ref[...] = ref[ref.shape[0] - count :]

    by_parity(lambda: put(even_ref), lambda: put(odd_ref))


def columns(first, count, tokens):
    return slice(first * tokens, (first + count) * tokens)


def grams_kernel(train_ref, *refs):
    *part_refs, out_ref = refs
    layers, tokens = train_ref.shape[1], train_ref.shape[3]
    for layer in range(layers):
        for index in range(2):
            for group in groups(train_ref):
                rows = slice(group.start * tokens, group.stop * tokens)
                out_ref[layer, index, rows] = gram(train_ref, part_refs, layer, index, group)


def add_kernel(train_ref, far_ref, near_ref, grams_ref, out_ref):
    layers, tokens, features = train_ref.shape[1], train_ref.shape[3], train_ref.shape[4]
    detour = columns(0, far_ref.shape[0], tokens)
    rest = slice(detour.stop, grams_ref.shape[-1])

    def add(last_ref):
        begin = features - last_ref.shape[-1]
        for layer in range(layers):
            for index in range(2):
                for group in groups(train_ref):
                    rows = slice(group.start * tokens, group.stop * tokens)
                    out_ref[layer, index, rows, detour] = grams_ref[layer, index, rows, detour] + gram(
                        train_ref, [last_ref], layer, index, group, begin
                    )

    out_ref[..., rest] = grams_ref[..., rest]
    by_parity(lambda: add(far_ref), lambda: add(near_ref))


def middle_kernel(train_ref, part_ref, grams_ref, ends_ref, out_ref):
    layers, tokens, features = train_ref.shape[1], train_ref.shape[3], train_ref.shape[4]
    depth = part_ref.shape[-1]
    detour = columns(0, out_ref.shape[0], tokens)
    rest = slice(detour.stop, grams_ref.shape[-1])
    sums = []
    for group in groups(train_ref):
        rows = slice(group.start * tokens, group.stop * tokens)
        product = 0.0
        for layer in range(layers):
            totals = [
                grams_ref[layer, index, rows]
                + gram(train_ref, [part_ref], layer, index, group, features - 2 * depth)
                for index in range(2)
            ]
            product = product + totals[0][:, detour] * totals[1][:, detour]
            for index in range(2):
                ends_ref[layer, index, rows] = totals[index][:, rest]
        sums.append(token_sums(product, tokens))
    out_ref[...] = example_sums(jnp.concatenate(sums, axis=0), tokens)


def last_kernel(train_ref, end_ref, ends_ref, own_ref, first_ref, second_ref, out_ref):
    layers, tokens, features = train_ref.shape[1], train_ref.shape[3], train_ref.shape[4]
    start = features - end_ref.shape[-1]
    sums = []
    for group in groups(train_ref):
        rows = slice(group.start * tokens, group.stop * tokens)
        product = 0.0
        for layer in range(layers):
            act, grad = (
                ends_ref[layer, index, rows] + gram(train_ref, [end_ref], layer, index, group, start)
                for index in range(2)
            )
            product = product + act * grad
        sums.append(token_sums(product, tokens))
    ready = first_ref.shape[0]
    out_ref[0] = own_ref[...]
    out_ref[1, :ready] = first_ref[...]
    out_ref[1, ready:] = example_sums(jnp.concatenate(sums, axis=0), tokens)
    out_ref[2] = second_ref[...]


def summed(rows, axis):
    if lax.axis_size(axis) != 2:
        return lax.psum(rows, axis)
    return rows + permuted(rows, axis, lambda i: i ^ 1)


def local(train, val):
    examples, layers, _, tokens, features = train.shape
    count = val.shape[0]
    cuts = CUTS
    depth = features // cuts
    work = 4 * examples * count * layers * tokens * tokens * features
    part = jax.ShapeDtypeStruct(val.shape[:-1] + (depth,), val.dtype)
    small = jax.ShapeDtypeStruct((1,) + part.shape[1:], val.dtype)
    rows = jax.ShapeDtypeStruct((count, examples), jnp.float32)
    grams = jax.ShapeDtypeStruct((layers, 2, examples * tokens, count * tokens), jnp.float32)

    detour = val[: count - 1, ..., (cuts - 1) * depth :]
    parts = [val[..., :depth], *call(cut_kernel, [part] * (cuts - 1), [VMEM], [val])]
    second = [permuted(x, "blk", lambda i: i + 2) for x in parts]
    near_last = permuted(detour, "blk", lambda i: i ^ 1)
    far_last = permuted(near_last, "blk", lambda i: i + 2)
    first = []
    for c in range(cuts - 1):
        operands = [parts[c], second[c]] + ([near_last] if c == 1 else [])
        picked = call(pick_kernel, part, [VMEM] * len(operands), operands)
        first.append(permuted(picked, "blk", lambda i: i ^ 1))
    picked = call(pick_last_kernel, small, [VMEM] * 2, [parts[-1], second[-1]])
    end = permuted(picked, "blk", lambda i: i ^ 1)

    operands = [train] + parts
    own = call(scores_kernel, rows, [VMEM] * len(operands), operands, work)
    operands = [train] + second
    far = call(scores_kernel, rows, [VMEM] * len(operands), operands, work)
    sums = call(grams_kernel, grams, [VMEM] * (cuts - 1), [train] + first[:-1], work // 2)
    sums = call(add_kernel, grams, [VMEM] * 4, [train, far_last, near_last, sums], 5 * work // 4)
    ends = jax.ShapeDtypeStruct(grams.shape[:-1] + (tokens,), jnp.float32)
    ready = jax.ShapeDtypeStruct((count - 1, examples), jnp.float32)
    operands = [train, first[-1], sums]
    ends, ready = call(middle_kernel, [ends, ready], [VMEM] * len(operands), operands, work // 4)
    out = jax.ShapeDtypeStruct((3,) + rows.shape, jnp.float32)
    operands = [train, end, ends, own, ready, far]
    partial_rows = call(last_kernel, out, [VMEM] * len(operands), operands, work // 16)
    return summed(partial_rows, "layer").transpose(2, 0, 1)


def solution(mesh):
    return jax.shard_map(
        local,
        mesh=mesh,
        in_specs=(P("blk", "layer", None, None, None), P("blk", "layer", None, None, None)),
        out_specs=P("blk", None, None),
        check_vma=False,
    )
```

```python
import functools

import jax
import jax.numpy as jnp
from jax import lax
from jax.experimental import pallas as pl
from jax.experimental.pallas import tpu as pltpu
from jax.sharding import PartitionSpec as P

CUTS = 4
GROUP = 4

VMEM = pl.BlockSpec(memory_space=pltpu.VMEM)


def permuted(block, axis, target):
    size = lax.axis_size(axis)
    return lax.ppermute(block, axis, [(i, target(i) % size) for i in range(size)])


def call(kernel, out_shape, specs, operands, flops=0, scratch=(), vmem=16 << 20):
    shapes = list(operands) + jax.tree.leaves(out_shape)
    return pl.pallas_call(
        kernel,
        out_shape=out_shape,
        in_specs=specs,
        out_specs=jax.tree.map(lambda _: VMEM, out_shape),
        scratch_shapes=scratch,
        compiler_params=pltpu.CompilerParams(vmem_limit_bytes=vmem),
        cost_estimate=pl.CostEstimate(
            flops=flops,
            bytes_accessed=sum(x.size * x.dtype.itemsize for x in shapes),
            transcendentals=0,
        ),
    )(*operands)


def groups(train_ref):
    examples = train_ref.shape[0]
    size = GROUP if examples % GROUP == 0 else 1
    return [slice(first, first + size) for first in range(0, examples, size)]


def gram(train_ref, val_refs, layer, index, group, start=0):
    total = 0.0
    for ref in val_refs:
        depth = ref.shape[-1]
        train = train_ref[group, layer, index, :, start : start + depth].reshape(-1, depth)
        val = ref[:, layer, index].reshape(-1, depth)
        total = total + lax.dot_general(
            train, val, (((1,), (1,)), ((), ())), preferred_element_type=jnp.float32
        )
        start += depth
    return total


def token_sums(product, tokens):
    return jnp.sum(product.reshape(-1, tokens, product.shape[-1]), axis=1)


def example_sums(by_token, tokens):
    count = by_token.shape[-1] // tokens
    shape = (count, by_token.shape[-1])
    token = lax.broadcasted_iota(jnp.int32, shape, 1) // tokens
    mine = (token == lax.broadcasted_iota(jnp.int32, shape, 0)).astype(jnp.float32)
    return lax.dot_general(
        mine, by_token, (((1,), (1,)), ((), ())),
        precision=lax.Precision.HIGHEST, preferred_element_type=jnp.float32,
    )


def scores(train_ref, val_refs):
    layers, tokens = train_ref.shape[1], train_ref.shape[3]
    sums = []
    for group in groups(train_ref):
        product = 0.0
        for layer in range(layers):
            product = product + gram(train_ref, val_refs, layer, 0, group) * gram(
                train_ref, val_refs, layer, 1, group
            )
        sums.append(token_sums(product, tokens))
    return example_sums(jnp.concatenate(sums, axis=0), tokens)


def cut_kernel(val_ref, *part_refs):
    for c, ref in enumerate(part_refs, 1):
        depth = ref.shape[-1]
        ref[...] = val_ref[..., c * depth : (c + 1) * depth]


def scores_kernel(train_ref, *refs):
    *val_refs, out_ref = refs
    out_ref[...] = scores(train_ref, val_refs)


def by_parity(even, odd):
    parity = lax.rem(lax.axis_index("blk"), 2)
    pl.when(parity == 0)(even)
    pl.when(parity == 1)(odd)


def pick_kernel(even_ref, odd_ref, *refs):
    out_ref = refs[-1]

    def put(ref):
        out_ref[...] = ref[...]

    by_parity(lambda: put(even_ref), lambda: put(odd_ref))


def pick_last_kernel(even_ref, odd_ref, *refs):
    out_ref = refs[-1]
    count = out_ref.shape[0]

    def put(ref):
        out_ref[...] = ref[ref.shape[0] - count :]

    by_parity(lambda: put(even_ref), lambda: put(odd_ref))


def columns(first, count, tokens):
    return slice(first * tokens, (first + count) * tokens)


def grams_kernel(train_ref, *refs):
    *part_refs, out_ref = refs
    layers, tokens = train_ref.shape[1], train_ref.shape[3]
    for layer in range(layers):
        for index in range(2):
            for group in groups(train_ref):
                rows = slice(group.start * tokens, group.stop * tokens)
                out_ref[layer, index, rows] = gram(train_ref, part_refs, layer, index, group)


def second_kernel(train_ref, part_ref, grams_ref, _, out_ref):
    layers, tokens, features = train_ref.shape[1], train_ref.shape[3], train_ref.shape[4]
    start = features - part_ref.shape[-1]
    sums = []
    for group in groups(train_ref):
        rows = slice(group.start * tokens, group.stop * tokens)
        product = 0.0
        for layer in range(layers):
            act, grad = (
                grams_ref[layer, index, rows] + gram(train_ref, [part_ref], layer, index, group, start)
                for index in range(2)
            )
            product = product + act * grad
        sums.append(token_sums(product, tokens))
    out_ref[...] = example_sums(jnp.concatenate(sums, axis=0), tokens)


def add_kernel(train_ref, far_ref, near_ref, grams_ref, _, out_ref):
    layers, tokens, features = train_ref.shape[1], train_ref.shape[3], train_ref.shape[4]
    detour = columns(0, far_ref.shape[0], tokens)
    rest = slice(detour.stop, grams_ref.shape[-1])

    def add(last_ref):
        begin = features - last_ref.shape[-1]
        for layer in range(layers):
            for index in range(2):
                for group in groups(train_ref):
                    rows = slice(group.start * tokens, group.stop * tokens)
                    out_ref[layer, index, rows, detour] = grams_ref[layer, index, rows, detour] + gram(
                        train_ref, [last_ref], layer, index, group, begin
                    )

    out_ref[..., rest] = grams_ref[..., rest]
    by_parity(lambda: add(far_ref), lambda: add(near_ref))


def middle_kernel(train_ref, part_ref, grams_ref, ends_ref, out_ref):
    layers, tokens, features = train_ref.shape[1], train_ref.shape[3], train_ref.shape[4]
    depth = part_ref.shape[-1]
    detour = columns(0, out_ref.shape[0], tokens)
    rest = slice(detour.stop, grams_ref.shape[-1])
    sums = []
    for group in groups(train_ref):
        rows = slice(group.start * tokens, group.stop * tokens)
        product = 0.0
        for layer in range(layers):
            totals = [
                grams_ref[layer, index, rows]
                + gram(train_ref, [part_ref], layer, index, group, features - 2 * depth)
                for index in range(2)
            ]
            product = product + totals[0][:, detour] * totals[1][:, detour]
            for index in range(2):
                ends_ref[layer, index, rows] = totals[index][:, rest]
        sums.append(token_sums(product, tokens))
    out_ref[...] = example_sums(jnp.concatenate(sums, axis=0), tokens)


def last_kernel(train_ref, end_ref, ends_ref, own_ref, first_ref, second_ref, out_ref):
    layers, tokens, features = train_ref.shape[1], train_ref.shape[3], train_ref.shape[4]
    start = features - end_ref.shape[-1]
    sums = []
    for group in groups(train_ref):
        rows = slice(group.start * tokens, group.stop * tokens)
        product = 0.0
        for layer in range(layers):
            act, grad = (
                ends_ref[layer, index, rows] + gram(train_ref, [end_ref], layer, index, group, start)
                for index in range(2)
            )
            product = product + act * grad
        sums.append(token_sums(product, tokens))
    ready = first_ref.shape[0]
    out_ref[0] = own_ref[...]
    out_ref[1, :ready] = first_ref[...]
    out_ref[1, ready:] = example_sums(jnp.concatenate(sums, axis=0), tokens)
    out_ref[2] = second_ref[...]


def summed(rows, axis):
    if lax.axis_size(axis) != 2:
        return lax.psum(rows, axis)
    return rows + permuted(rows, axis, lambda i: i ^ 1)


def local(train, val):
    examples, layers, _, tokens, features = train.shape
    count = val.shape[0]
    cuts = CUTS
    depth = features // cuts
    work = 4 * examples * count * layers * tokens * tokens * features
    part = jax.ShapeDtypeStruct(val.shape[:-1] + (depth,), val.dtype)
    small = jax.ShapeDtypeStruct((1,) + part.shape[1:], val.dtype)
    rows = jax.ShapeDtypeStruct((count, examples), jnp.float32)
    grams = jax.ShapeDtypeStruct((layers, 2, examples * tokens, count * tokens), jnp.float32)

    detour = val[: count - 1, ..., (cuts - 1) * depth :]
    parts = [val[..., :depth], *call(cut_kernel, [part] * (cuts - 1), [VMEM], [val])]
    second = [permuted(x, "blk", lambda i: i + 2) for x in parts]
    near_last = permuted(detour, "blk", lambda i: i ^ 1)
    far_last = permuted(near_last, "blk", lambda i: i + 2)
    first = []
    for c in range(cuts - 1):
        operands = [parts[c], second[c]] + ([near_last] if c == 1 else [])
        picked = call(pick_kernel, part, [VMEM] * len(operands), operands)
        first.append(permuted(picked, "blk", lambda i: i ^ 1))
    sums = call(grams_kernel, grams, [VMEM] * (cuts - 1), [train] + first[:-1], work // 2)
    far = call(grams_kernel, grams, [VMEM] * cuts, [train] + second[:-1], work)
    operands = [parts[-1], second[-1], sums, far]
    picked = call(pick_last_kernel, small, [VMEM] * len(operands), operands)
    end = permuted(picked, "blk", lambda i: i ^ 1)

    own = call(scores_kernel, rows, [VMEM] * (1 + cuts), [train] + parts, work)
    operands = [train, second[-1], far, picked]
    far = call(second_kernel, rows, [VMEM] * len(operands), operands, work // 4)
    sums = call(add_kernel, grams, [VMEM] * 5, [train, far_last, near_last, sums, far], work)
    ends = jax.ShapeDtypeStruct(grams.shape[:-1] + (tokens,), jnp.float32)
    ready = jax.ShapeDtypeStruct((count - 1, examples), jnp.float32)
    operands = [train, first[-1], sums]
    ends, ready = call(middle_kernel, [ends, ready], [VMEM] * len(operands), operands, work // 4)
    out = jax.ShapeDtypeStruct((3,) + rows.shape, jnp.float32)
    operands = [train, end, ends, own, ready, far]
    partial_rows = call(last_kernel, out, [VMEM] * len(operands), operands, work // 16)
    return summed(partial_rows, "layer").transpose(2, 0, 1)


def solution(mesh):
    return jax.shard_map(
        local,
        mesh=mesh,
        in_specs=(P("blk", "layer", None, None, None), P("blk", "layer", None, None, None)),
        out_specs=P("blk", None, None),
        check_vma=False,
    )
```

```python
import functools

import jax
import jax.numpy as jnp
from jax import lax
from jax.experimental import pallas as pl
from jax.experimental.pallas import tpu as pltpu
from jax.sharding import PartitionSpec as P

CUTS = 4
GROUP = 4

VMEM = pl.BlockSpec(memory_space=pltpu.VMEM)


def permuted(block, axis, target):
    size = lax.axis_size(axis)
    return lax.ppermute(block, axis, [(i, target(i) % size) for i in range(size)])


def call(kernel, out_shape, specs, operands, flops=0, scratch=(), vmem=16 << 20):
    shapes = list(operands) + jax.tree.leaves(out_shape)
    return pl.pallas_call(
        kernel,
        out_shape=out_shape,
        in_specs=specs,
        out_specs=jax.tree.map(lambda _: VMEM, out_shape),
        scratch_shapes=scratch,
        compiler_params=pltpu.CompilerParams(vmem_limit_bytes=vmem),
        cost_estimate=pl.CostEstimate(
            flops=flops,
            bytes_accessed=sum(x.size * x.dtype.itemsize for x in shapes),
            transcendentals=0,
        ),
    )(*operands)


def groups(train_ref):
    examples = train_ref.shape[0]
    size = GROUP if examples % GROUP == 0 else 1
    return [slice(first, first + size) for first in range(0, examples, size)]


def gram(train_ref, val_refs, layer, index, group, start=0):
    total = 0.0
    for ref in val_refs:
        depth = ref.shape[-1]
        train = train_ref[group, layer, index, :, start : start + depth].reshape(-1, depth)
        val = ref[:, layer, index].reshape(-1, depth)
        total = total + lax.dot_general(
            train, val, (((1,), (1,)), ((), ())), preferred_element_type=jnp.float32
        )
        start += depth
    return total


def token_sums(product, tokens):
    return jnp.sum(product.reshape(-1, tokens, product.shape[-1]), axis=1)


def example_sums(by_token, tokens):
    count = by_token.shape[-1] // tokens
    shape = (count, by_token.shape[-1])
    token = lax.broadcasted_iota(jnp.int32, shape, 1) // tokens
    mine = (token == lax.broadcasted_iota(jnp.int32, shape, 0)).astype(jnp.float32)
    return lax.dot_general(
        mine, by_token, (((1,), (1,)), ((), ())),
        precision=lax.Precision.HIGHEST, preferred_element_type=jnp.float32,
    )


def scores(train_ref, val_refs):
    layers, tokens = train_ref.shape[1], train_ref.shape[3]
    sums = []
    for group in groups(train_ref):
        product = 0.0
        for layer in range(layers):
            product = product + gram(train_ref, val_refs, layer, 0, group) * gram(
                train_ref, val_refs, layer, 1, group
            )
        sums.append(token_sums(product, tokens))
    return example_sums(jnp.concatenate(sums, axis=0), tokens)


def cut_kernel(val_ref, *part_refs):
    for c, ref in enumerate(part_refs, 1):
        depth = ref.shape[-1]
        ref[...] = val_ref[..., c * depth : (c + 1) * depth]


def scores_kernel(train_ref, *refs):
    *val_refs, out_ref = refs
    out_ref[...] = scores(train_ref, val_refs)


def by_parity(even, odd):
    parity = lax.rem(lax.axis_index("blk"), 2)
    pl.when(parity == 0)(even)
    pl.when(parity == 1)(odd)


def pick_kernel(even_ref, odd_ref, *refs):
    out_ref = refs[-1]

    def put(ref):
        out_ref[...] = ref[...]

    by_parity(lambda: put(even_ref), lambda: put(odd_ref))


def pick_last_kernel(even_ref, odd_ref, *refs):
    out_ref = refs[-1]
    count = out_ref.shape[0]

    def put(ref):
        out_ref[...] = ref[ref.shape[0] - count :]

    by_parity(lambda: put(even_ref), lambda: put(odd_ref))


def columns(first, count, tokens):
    return slice(first * tokens, (first + count) * tokens)


def grams_kernel(train_ref, *refs):
    *part_refs, out_ref = refs
    layers, tokens = train_ref.shape[1], train_ref.shape[3]
    for layer in range(layers):
        for index in range(2):
            for group in groups(train_ref):
                rows = slice(group.start * tokens, group.stop * tokens)
                out_ref[layer, index, rows] = gram(train_ref, part_refs, layer, index, group)


def second_kernel(train_ref, part_ref, grams_ref, out_ref):
    layers, tokens, features = train_ref.shape[1], train_ref.shape[3], train_ref.shape[4]
    start = features - part_ref.shape[-1]
    sums = []
    for group in groups(train_ref):
        rows = slice(group.start * tokens, group.stop * tokens)
        product = 0.0
        for layer in range(layers):
            act, grad = (
                grams_ref[layer, index, rows] + gram(train_ref, [part_ref], layer, index, group, start)
                for index in range(2)
            )
            product = product + act * grad
        sums.append(token_sums(product, tokens))
    out_ref[...] = example_sums(jnp.concatenate(sums, axis=0), tokens)


def add_kernel(train_ref, far_ref, near_ref, grams_ref, out_ref):
    layers, tokens, features = train_ref.shape[1], train_ref.shape[3], train_ref.shape[4]
    detour = columns(0, far_ref.shape[0], tokens)
    rest = slice(detour.stop, grams_ref.shape[-1])

    def add(last_ref):
        begin = features - last_ref.shape[-1]
        for layer in range(layers):
            for index in range(2):
                for group in groups(train_ref):
                    rows = slice(group.start * tokens, group.stop * tokens)
                    out_ref[layer, index, rows, detour] = grams_ref[layer, index, rows, detour] + gram(
                        train_ref, [last_ref], layer, index, group, begin
                    )

    out_ref[..., rest] = grams_ref[..., rest]
    by_parity(lambda: add(far_ref), lambda: add(near_ref))


def middle_kernel(train_ref, part_ref, grams_ref, ends_ref, out_ref):
    layers, tokens, features = train_ref.shape[1], train_ref.shape[3], train_ref.shape[4]
    depth = part_ref.shape[-1]
    detour = columns(0, out_ref.shape[0], tokens)
    rest = slice(detour.stop, grams_ref.shape[-1])
    sums = []
    for group in groups(train_ref):
        rows = slice(group.start * tokens, group.stop * tokens)
        product = 0.0
        for layer in range(layers):
            totals = [
                grams_ref[layer, index, rows]
                + gram(train_ref, [part_ref], layer, index, group, features - 2 * depth)
                for index in range(2)
            ]
            product = product + totals[0][:, detour] * totals[1][:, detour]
            for index in range(2):
                ends_ref[layer, index, rows] = totals[index][:, rest]
        sums.append(token_sums(product, tokens))
    out_ref[...] = example_sums(jnp.concatenate(sums, axis=0), tokens)


def last_kernel(train_ref, end_ref, ends_ref, own_ref, first_ref, second_ref, out_ref):
    layers, tokens, features = train_ref.shape[1], train_ref.shape[3], train_ref.shape[4]
    start = features - end_ref.shape[-1]
    sums = []
    for group in groups(train_ref):
        rows = slice(group.start * tokens, group.stop * tokens)
        product = 0.0
        for layer in range(layers):
            act, grad = (
                ends_ref[layer, index, rows] + gram(train_ref, [end_ref], layer, index, group, start)
                for index in range(2)
            )
            product = product + act * grad
        sums.append(token_sums(product, tokens))
    ready = first_ref.shape[0]
    out_ref[0] = own_ref[...]
    out_ref[1, :ready] = first_ref[...]
    out_ref[1, ready:] = example_sums(jnp.concatenate(sums, axis=0), tokens)
    out_ref[2] = second_ref[...]


def summed(rows, axis):
    if lax.axis_size(axis) != 2:
        return lax.psum(rows, axis)
    return rows + permuted(rows, axis, lambda i: i ^ 1)


def local(train, val):
    examples, layers, _, tokens, features = train.shape
    count = val.shape[0]
    cuts = CUTS
    depth = features // cuts
    work = 4 * examples * count * layers * tokens * tokens * features
    part = jax.ShapeDtypeStruct(val.shape[:-1] + (depth,), val.dtype)
    small = jax.ShapeDtypeStruct((1,) + part.shape[1:], val.dtype)
    rows = jax.ShapeDtypeStruct((count, examples), jnp.float32)
    grams = jax.ShapeDtypeStruct((layers, 2, examples * tokens, count * tokens), jnp.float32)

    detour = val[: count - 1, ..., (cuts - 1) * depth :]
    parts = [val[..., :depth], *call(cut_kernel, [part] * (cuts - 1), [VMEM], [val])]
    second = [permuted(x, "blk", lambda i: i + 2) for x in parts]
    near_last = permuted(detour, "blk", lambda i: i ^ 1)
    far_last = permuted(near_last, "blk", lambda i: i + 2)
    first = []
    for c in range(cuts - 1):
        operands = [parts[c], second[c]] + ([near_last] if c == 1 else [])
        picked = call(pick_kernel, part, [VMEM] * len(operands), operands)
        first.append(permuted(picked, "blk", lambda i: i ^ 1))
    sums = call(grams_kernel, grams, [VMEM] * (cuts - 1), [train] + first[:-1], work // 2)
    far = call(grams_kernel, grams, [VMEM] * cuts, [train] + second[:-1], work)
    operands = [parts[-1], second[-1], far]
    picked = call(pick_last_kernel, small, [VMEM] * len(operands), operands)
    end = permuted(picked, "blk", lambda i: i ^ 1)

    own = call(scores_kernel, rows, [VMEM] * (1 + cuts), [train] + parts, work)
    far = call(second_kernel, rows, [VMEM] * 3, [train, second[-1], far], work // 4)
    sums = call(add_kernel, grams, [VMEM] * 4, [train, far_last, near_last, sums], 5 * work // 4)
    ends = jax.ShapeDtypeStruct(grams.shape[:-1] + (tokens,), jnp.float32)
    ready = jax.ShapeDtypeStruct((count - 1, examples), jnp.float32)
    operands = [train, first[-1], sums]
    ends, ready = call(middle_kernel, [ends, ready], [VMEM] * len(operands), operands, work // 4)
    out = jax.ShapeDtypeStruct((3,) + rows.shape, jnp.float32)
    operands = [train, end, ends, own, ready, far]
    partial_rows = call(last_kernel, out, [VMEM] * len(operands), operands, work // 16)
    return summed(partial_rows, "layer").transpose(2, 0, 1)


def solution(mesh):
    return jax.shard_map(
        local,
        mesh=mesh,
        in_specs=(P("blk", "layer", None, None, None), P("blk", "layer", None, None, None)),
        out_specs=P("blk", None, None),
        check_vma=False,
    )
```

```python
import functools

import jax
import jax.numpy as jnp
from jax import lax
from jax.experimental import pallas as pl
from jax.experimental.pallas import tpu as pltpu
from jax.sharding import PartitionSpec as P

CUTS = 4
GROUP = 4

VMEM = pl.BlockSpec(memory_space=pltpu.VMEM)


def permuted(block, axis, target):
    size = lax.axis_size(axis)
    return lax.ppermute(block, axis, [(i, target(i) % size) for i in range(size)])


def call(kernel, out_shape, specs, operands, flops=0, scratch=(), vmem=16 << 20):
    shapes = list(operands) + jax.tree.leaves(out_shape)
    return pl.pallas_call(
        kernel,
        out_shape=out_shape,
        in_specs=specs,
        out_specs=jax.tree.map(lambda _: VMEM, out_shape),
        scratch_shapes=scratch,
        compiler_params=pltpu.CompilerParams(vmem_limit_bytes=vmem),
        cost_estimate=pl.CostEstimate(
            flops=flops,
            bytes_accessed=sum(x.size * x.dtype.itemsize for x in shapes),
            transcendentals=0,
        ),
    )(*operands)


def groups(train_ref):
    examples = train_ref.shape[0]
    size = GROUP if examples % GROUP == 0 else 1
    return [slice(first, first + size) for first in range(0, examples, size)]


def gram(train_ref, val_refs, layer, index, group, start=0):
    total = 0.0
    for ref in val_refs:
        depth = ref.shape[-1]
        train = train_ref[group, layer, index, :, start : start + depth].reshape(-1, depth)
        val = ref[:, layer, index].reshape(-1, depth)
        total = total + lax.dot_general(
            train, val, (((1,), (1,)), ((), ())), preferred_element_type=jnp.float32
        )
        start += depth
    return total


def token_sums(product, tokens):
    return jnp.sum(product.reshape(-1, tokens, product.shape[-1]), axis=1)


def example_sums(by_token, tokens):
    count = by_token.shape[-1] // tokens
    shape = (count, by_token.shape[-1])
    token = lax.broadcasted_iota(jnp.int32, shape, 1) // tokens
    mine = (token == lax.broadcasted_iota(jnp.int32, shape, 0)).astype(jnp.bfloat16)
    total, rest = 0.0, by_token
    for _ in range(3):
        piece = rest.astype(jnp.bfloat16)
        rest = rest - piece.astype(jnp.float32)
        total = total + lax.dot_general(
            mine, piece, (((1,), (1,)), ((), ())), preferred_element_type=jnp.float32
        )
    return total


def scores(train_ref, val_refs):
    layers, tokens = train_ref.shape[1], train_ref.shape[3]
    sums = []
    for group in groups(train_ref):
        product = 0.0
        for layer in range(layers):
            product = product + gram(train_ref, val_refs, layer, 0, group) * gram(
                train_ref, val_refs, layer, 1, group
            )
        sums.append(token_sums(product, tokens))
    return example_sums(jnp.concatenate(sums, axis=0), tokens)


def cut_kernel(val_ref, *part_refs):
    for c, ref in enumerate(part_refs, 1):
        depth = ref.shape[-1]
        ref[...] = val_ref[..., c * depth : (c + 1) * depth]


def scores_kernel(train_ref, *refs):
    *val_refs, out_ref = refs
    out_ref[...] = scores(train_ref, val_refs)


def by_parity(even, odd):
    parity = lax.rem(lax.axis_index("blk"), 2)
    pl.when(parity == 0)(even)
    pl.when(parity == 1)(odd)


def pick_kernel(even_ref, odd_ref, *refs):
    out_ref = refs[-1]

    def put(ref):
        out_ref[...] = ref[...]

    by_parity(lambda: put(even_ref), lambda: put(odd_ref))


def pick_last_kernel(even_ref, odd_ref, *refs):
    out_ref = refs[-1]
    count = out_ref.shape[0]

    def put(ref):
        out_ref[...] = ref[ref.shape[0] - count :]

    by_parity(lambda: put(even_ref), lambda: put(odd_ref))


def columns(first, count, tokens):
    return slice(first * tokens, (first + count) * tokens)


def grams_kernel(train_ref, *refs):
    *part_refs, out_ref = refs
    layers, tokens = train_ref.shape[1], train_ref.shape[3]
    for layer in range(layers):
        for index in range(2):
            for group in groups(train_ref):
                rows = slice(group.start * tokens, group.stop * tokens)
                out_ref[layer, index, rows] = gram(train_ref, part_refs, layer, index, group)


def second_kernel(train_ref, part_ref, grams_ref, out_ref):
    layers, tokens, features = train_ref.shape[1], train_ref.shape[3], train_ref.shape[4]
    start = features - part_ref.shape[-1]
    sums = []
    for group in groups(train_ref):
        rows = slice(group.start * tokens, group.stop * tokens)
        product = 0.0
        for layer in range(layers):
            act, grad = (
                grams_ref[layer, index, rows] + gram(train_ref, [part_ref], layer, index, group, start)
                for index in range(2)
            )
            product = product + act * grad
        sums.append(token_sums(product, tokens))
    out_ref[...] = example_sums(jnp.concatenate(sums, axis=0), tokens)


def middle_kernel(train_ref, part_ref, last_ref, grams_ref, ends_ref, out_ref):
    layers, tokens, features = train_ref.shape[1], train_ref.shape[3], train_ref.shape[4]
    depth = part_ref.shape[-1]
    detour = columns(0, out_ref.shape[0], tokens)
    rest = slice(detour.stop, grams_ref.shape[-1])
    sums = []
    for group in groups(train_ref):
        rows = slice(group.start * tokens, group.stop * tokens)
        product = 0.0
        for layer in range(layers):
            totals = [
                grams_ref[layer, index, rows]
                + gram(train_ref, [part_ref], layer, index, group, features - 2 * depth)
                for index in range(2)
            ]
            act, grad = (
                totals[index][:, detour]
                + gram(train_ref, [last_ref], layer, index, group, features - depth)
                for index in range(2)
            )
            product = product + act * grad
            for index in range(2):
                ends_ref[layer, index, rows] = totals[index][:, rest]
        sums.append(token_sums(product, tokens))
    out_ref[...] = example_sums(jnp.concatenate(sums, axis=0), tokens)


def last_kernel(train_ref, end_ref, ends_ref, own_ref, first_ref, second_ref, out_ref):
    layers, tokens, features = train_ref.shape[1], train_ref.shape[3], train_ref.shape[4]
    start = features - end_ref.shape[-1]
    sums = []
    for group in groups(train_ref):
        rows = slice(group.start * tokens, group.stop * tokens)
        product = 0.0
        for layer in range(layers):
            act, grad = (
                ends_ref[layer, index, rows] + gram(train_ref, [end_ref], layer, index, group, start)
                for index in range(2)
            )
            product = product + act * grad
        sums.append(token_sums(product, tokens))
    ready = first_ref.shape[0]
    out_ref[0] = own_ref[...]
    out_ref[1, :ready] = first_ref[...]
    out_ref[1, ready:] = example_sums(jnp.concatenate(sums, axis=0), tokens)
    out_ref[2] = second_ref[...]


def summed(rows, axis):
    if lax.axis_size(axis) != 2:
        return lax.psum(rows, axis)
    return rows + permuted(rows, axis, lambda i: i ^ 1)


def local(train, val):
    examples, layers, _, tokens, features = train.shape
    count = val.shape[0]
    cuts = CUTS
    depth = features // cuts
    work = 4 * examples * count * layers * tokens * tokens * features
    part = jax.ShapeDtypeStruct(val.shape[:-1] + (depth,), val.dtype)
    small = jax.ShapeDtypeStruct((1,) + part.shape[1:], val.dtype)
    rows = jax.ShapeDtypeStruct((count, examples), jnp.float32)
    grams = jax.ShapeDtypeStruct((layers, 2, examples * tokens, count * tokens), jnp.float32)

    detour = val[: count - 1, ..., (cuts - 1) * depth :]
    parts = [val[..., :depth], *call(cut_kernel, [part] * (cuts - 1), [VMEM], [val])]
    second = [permuted(x, "blk", lambda i: i + 2) for x in parts]
    near_last = permuted(detour, "blk", lambda i: i ^ 1)
    far_last = permuted(near_last, "blk", lambda i: i + 2)
    first = []
    for c in range(cuts - 1):
        operands = [parts[c], second[c]] + ([near_last] if c == 1 else [])
        picked = call(pick_kernel, part, [VMEM] * len(operands), operands)
        first.append(permuted(picked, "blk", lambda i: i ^ 1))
    sums = call(grams_kernel, grams, [VMEM] * (cuts - 1), [train] + first[:-1], work // 2)
    far = call(grams_kernel, grams, [VMEM] * cuts, [train] + second[:-1], work)
    operands = [parts[-1], second[-1], far]
    picked = call(pick_last_kernel, small, [VMEM] * len(operands), operands)
    end = permuted(picked, "blk", lambda i: i ^ 1)

    own = call(scores_kernel, rows, [VMEM] * (1 + cuts), [train] + parts, work)
    far = call(second_kernel, rows, [VMEM] * 3, [train, second[-1], far], work // 4)
    last = call(pick_kernel, detour, [VMEM] * 3, [far_last, near_last, sums], work)
    ends = jax.ShapeDtypeStruct(grams.shape[:-1] + (tokens,), jnp.float32)
    ready = jax.ShapeDtypeStruct((count - 1, examples), jnp.float32)
    operands = [train, first[-1], last, sums]
    ends, ready = call(middle_kernel, [ends, ready], [VMEM] * len(operands), operands, work // 4)
    out = jax.ShapeDtypeStruct((3,) + rows.shape, jnp.float32)
    operands = [train, end, ends, own, ready, far]
    partial_rows = call(last_kernel, out, [VMEM] * len(operands), operands, work // 16)
    return summed(partial_rows, "layer").transpose(2, 0, 1)


def solution(mesh):
    return jax.shard_map(
        local,
        mesh=mesh,
        in_specs=(P("blk", "layer", None, None, None), P("blk", "layer", None, None, None)),
        out_specs=P("blk", None, None),
        check_vma=False,
    )
```

```python
import functools

import jax
import jax.numpy as jnp
from jax import lax
from jax.experimental import pallas as pl
from jax.experimental.pallas import tpu as pltpu
from jax.sharding import PartitionSpec as P

CUTS = 4
GROUP = 12

VMEM = pl.BlockSpec(memory_space=pltpu.VMEM)


def permuted(block, axis, target):
    size = lax.axis_size(axis)
    return lax.ppermute(block, axis, [(i, target(i) % size) for i in range(size)])


def call(kernel, out_shape, specs, operands, flops=0, scratch=(), vmem=16 << 20):
    shapes = list(operands) + jax.tree.leaves(out_shape)
    return pl.pallas_call(
        kernel,
        out_shape=out_shape,
        in_specs=specs,
        out_specs=jax.tree.map(lambda _: VMEM, out_shape),
        scratch_shapes=scratch,
        compiler_params=pltpu.CompilerParams(vmem_limit_bytes=vmem),
        cost_estimate=pl.CostEstimate(
            flops=flops,
            bytes_accessed=sum(x.size * x.dtype.itemsize for x in shapes),
            transcendentals=0,
        ),
    )(*operands)


def groups(train_ref):
    examples = train_ref.shape[0]
    size = GROUP if examples % GROUP == 0 else 1
    return [slice(first, first + size) for first in range(0, examples, size)]


def gram(train_ref, val_refs, layer, index, group, start=0):
    total = 0.0
    for ref in val_refs:
        depth = ref.shape[-1]
        train = train_ref[group, layer, index, :, start : start + depth].reshape(-1, depth)
        val = ref[:, layer, index].reshape(-1, depth)
        total = total + lax.dot_general(
            train, val, (((1,), (1,)), ((), ())), preferred_element_type=jnp.float32
        )
        start += depth
    return total


def token_sums(product, tokens):
    return jnp.sum(product.reshape(-1, tokens, product.shape[-1]), axis=1)


def example_sums(by_token, tokens):
    count = by_token.shape[-1] // tokens
    shape = (count, by_token.shape[-1])
    token = lax.broadcasted_iota(jnp.int32, shape, 1) // tokens
    mine = (token == lax.broadcasted_iota(jnp.int32, shape, 0)).astype(jnp.bfloat16)
    total, rest = 0.0, by_token
    for _ in range(3):
        piece = rest.astype(jnp.bfloat16)
        rest = rest - piece.astype(jnp.float32)
        total = total + lax.dot_general(
            mine, piece, (((1,), (1,)), ((), ())), preferred_element_type=jnp.float32
        )
    return total


def scores(train_ref, val_refs):
    layers, tokens = train_ref.shape[1], train_ref.shape[3]
    sums = []
    for group in groups(train_ref):
        product = 0.0
        for layer in range(layers):
            product = product + gram(train_ref, val_refs, layer, 0, group) * gram(
                train_ref, val_refs, layer, 1, group
            )
        sums.append(token_sums(product, tokens))
    return example_sums(jnp.concatenate(sums, axis=0), tokens)


def cut_kernel(val_ref, *part_refs):
    for c, ref in enumerate(part_refs, 1):
        depth = ref.shape[-1]
        ref[...] = val_ref[..., c * depth : (c + 1) * depth]


def scores_kernel(train_ref, *refs):
    *val_refs, out_ref = refs
    out_ref[...] = scores(train_ref, val_refs)


def by_parity(even, odd):
    parity = lax.rem(lax.axis_index("blk"), 2)
    pl.when(parity == 0)(even)
    pl.when(parity == 1)(odd)


def pick_kernel(even_ref, odd_ref, *refs):
    out_ref = refs[-1]

    def put(ref):
        out_ref[...] = ref[...]

    by_parity(lambda: put(even_ref), lambda: put(odd_ref))


def pick_last_kernel(even_ref, odd_ref, *refs):
    out_ref = refs[-1]
    count = out_ref.shape[0]

    def put(ref):
        out_ref[...] = ref[ref.shape[0] - count :]

    by_parity(lambda: put(even_ref), lambda: put(odd_ref))


def columns(first, count, tokens):
    return slice(first * tokens, (first + count) * tokens)


def grams_kernel(train_ref, *refs):
    *part_refs, out_ref = refs
    layers, tokens = train_ref.shape[1], train_ref.shape[3]
    for layer in range(layers):
        for index in range(2):
            for group in groups(train_ref):
                rows = slice(group.start * tokens, group.stop * tokens)
                out_ref[layer, index, rows] = gram(train_ref, part_refs, layer, index, group)


def second_kernel(train_ref, part_ref, grams_ref, out_ref):
    layers, tokens, features = train_ref.shape[1], train_ref.shape[3], train_ref.shape[4]
    start = features - part_ref.shape[-1]
    sums = []
    for group in groups(train_ref):
        rows = slice(group.start * tokens, group.stop * tokens)
        product = 0.0
        for layer in range(layers):
            act, grad = (
                grams_ref[layer, index, rows] + gram(train_ref, [part_ref], layer, index, group, start)
                for index in range(2)
            )
            product = product + act * grad
        sums.append(token_sums(product, tokens))
    out_ref[...] = example_sums(jnp.concatenate(sums, axis=0), tokens)


def middle_kernel(train_ref, part_ref, last_ref, grams_ref, ends_ref, out_ref):
    layers, tokens, features = train_ref.shape[1], train_ref.shape[3], train_ref.shape[4]
    depth = part_ref.shape[-1]
    detour = columns(0, out_ref.shape[0], tokens)
    rest = slice(detour.stop, grams_ref.shape[-1])
    sums = []
    for group in groups(train_ref):
        rows = slice(group.start * tokens, group.stop * tokens)
        product = 0.0
        for layer in range(layers):
            totals = [
                grams_ref[layer, index, rows]
                + gram(train_ref, [part_ref], layer, index, group, features - 2 * depth)
                for index in range(2)
            ]
            act, grad = (
                totals[index][:, detour]
                + gram(train_ref, [last_ref], layer, index, group, features - depth)
                for index in range(2)
            )
            product = product + act * grad
            for index in range(2):
                ends_ref[layer, index, rows] = totals[index][:, rest]
        sums.append(token_sums(product, tokens))
    out_ref[...] = example_sums(jnp.concatenate(sums, axis=0), tokens)


def last_kernel(train_ref, end_ref, ends_ref, own_ref, first_ref, second_ref, out_ref):
    layers, tokens, features = train_ref.shape[1], train_ref.shape[3], train_ref.shape[4]
    start = features - end_ref.shape[-1]
    sums = []
    for group in groups(train_ref):
        rows = slice(group.start * tokens, group.stop * tokens)
        product = 0.0
        for layer in range(layers):
            act, grad = (
                ends_ref[layer, index, rows] + gram(train_ref, [end_ref], layer, index, group, start)
                for index in range(2)
            )
            product = product + act * grad
        sums.append(token_sums(product, tokens))
    ready = first_ref.shape[0]
    out_ref[0] = own_ref[...]
    out_ref[1, :ready] = first_ref[...]
    out_ref[1, ready:] = example_sums(jnp.concatenate(sums, axis=0), tokens)
    out_ref[2] = second_ref[...]


def summed(rows, axis):
    if lax.axis_size(axis) != 2:
        return lax.psum(rows, axis)
    return rows + permuted(rows, axis, lambda i: i ^ 1)


def local(train, val):
    examples, layers, _, tokens, features = train.shape
    count = val.shape[0]
    cuts = CUTS
    depth = features // cuts
    work = 4 * examples * count * layers * tokens * tokens * features
    part = jax.ShapeDtypeStruct(val.shape[:-1] + (depth,), val.dtype)
    small = jax.ShapeDtypeStruct((1,) + part.shape[1:], val.dtype)
    rows = jax.ShapeDtypeStruct((count, examples), jnp.float32)
    grams = jax.ShapeDtypeStruct((layers, 2, examples * tokens, count * tokens), jnp.float32)

    detour = val[: count - 1, ..., (cuts - 1) * depth :]
    parts = [val[..., :depth], *call(cut_kernel, [part] * (cuts - 1), [VMEM], [val])]
    second = [permuted(x, "blk", lambda i: i + 2) for x in parts]
    near_last = permuted(detour, "blk", lambda i: i ^ 1)
    far_last = permuted(near_last, "blk", lambda i: i + 2)
    first = []
    for c in range(cuts - 1):
        operands = [parts[c], second[c]] + ([near_last] if c == 1 else [])
        picked = call(pick_kernel, part, [VMEM] * len(operands), operands)
        first.append(permuted(picked, "blk", lambda i: i ^ 1))
    sums = call(grams_kernel, grams, [VMEM] * (cuts - 1), [train] + first[:-1], work // 2)
    far = call(grams_kernel, grams, [VMEM] * cuts, [train] + second[:-1], work)
    operands = [parts[-1], second[-1], far]
    picked = call(pick_last_kernel, small, [VMEM] * len(operands), operands)
    end = permuted(picked, "blk", lambda i: i ^ 1)

    own = call(scores_kernel, rows, [VMEM] * (1 + cuts), [train] + parts, work)
    far = call(second_kernel, rows, [VMEM] * 3, [train, second[-1], far], work // 4)
    last = call(pick_kernel, detour, [VMEM] * 3, [far_last, near_last, sums], work)
    ends = jax.ShapeDtypeStruct(grams.shape[:-1] + (tokens,), jnp.float32)
    ready = jax.ShapeDtypeStruct((count - 1, examples), jnp.float32)
    operands = [train, first[-1], last, sums]
    ends, ready = call(middle_kernel, [ends, ready], [VMEM] * len(operands), operands, work // 4)
    out = jax.ShapeDtypeStruct((3,) + rows.shape, jnp.float32)
    operands = [train, end, ends, own, ready, far]
    partial_rows = call(last_kernel, out, [VMEM] * len(operands), operands, work // 16)
    return summed(partial_rows, "layer").transpose(2, 0, 1)


def solution(mesh):
    return jax.shard_map(
        local,
        mesh=mesh,
        in_specs=(P("blk", "layer", None, None, None), P("blk", "layer", None, None, None)),
        out_specs=P("blk", None, None),
        check_vma=False,
    )
```

```python
import functools

import jax
import jax.numpy as jnp
from jax import lax
from jax.experimental import pallas as pl
from jax.experimental.pallas import tpu as pltpu
from jax.sharding import PartitionSpec as P

CUTS = 4
GROUP = 4

VMEM = pl.BlockSpec(memory_space=pltpu.VMEM)
HBM = pl.BlockSpec(memory_space=pltpu.HBM)


def permuted(block, axis, target):
    size = lax.axis_size(axis)
    return lax.ppermute(block, axis, [(i, target(i) % size) for i in range(size)])


def call(kernel, out_shape, specs, operands, flops=0, scratch=(), vmem=16 << 20):
    shapes = list(operands) + jax.tree.leaves(out_shape)
    return pl.pallas_call(
        kernel,
        out_shape=out_shape,
        in_specs=specs,
        out_specs=jax.tree.map(lambda _: VMEM, out_shape),
        scratch_shapes=scratch,
        compiler_params=pltpu.CompilerParams(vmem_limit_bytes=vmem),
        cost_estimate=pl.CostEstimate(
            flops=flops,
            bytes_accessed=sum(x.size * x.dtype.itemsize for x in shapes),
            transcendentals=0,
        ),
    )(*operands)


def groups(train_ref):
    examples = train_ref.shape[0]
    size = GROUP if examples % GROUP == 0 else 1
    return [slice(first, first + size) for first in range(0, examples, size)]


def gram(train_ref, val_refs, layer, index, group, start=0):
    total = 0.0
    for ref in val_refs:
        depth = ref.shape[-1]
        train = train_ref[group, layer, index, :, start : start + depth].reshape(-1, depth)
        val = ref[:, layer, index].reshape(-1, depth)
        total = total + lax.dot_general(
            train, val, (((1,), (1,)), ((), ())), preferred_element_type=jnp.float32
        )
        start += depth
    return total


def token_sums(product, tokens):
    return jnp.sum(product.reshape(-1, tokens, product.shape[-1]), axis=1)


def example_sums(by_token, tokens):
    count = by_token.shape[-1] // tokens
    shape = (count, by_token.shape[-1])
    token = lax.broadcasted_iota(jnp.int32, shape, 1) // tokens
    mine = (token == lax.broadcasted_iota(jnp.int32, shape, 0)).astype(jnp.bfloat16)
    total, rest = 0.0, by_token
    for _ in range(3):
        piece = rest.astype(jnp.bfloat16)
        rest = rest - piece.astype(jnp.float32)
        total = total + lax.dot_general(
            mine, piece, (((1,), (1,)), ((), ())), preferred_element_type=jnp.float32
        )
    return total


def scores(train_ref, val_refs):
    layers, tokens = train_ref.shape[1], train_ref.shape[3]
    sums = []
    for group in groups(train_ref):
        product = 0.0
        for layer in range(layers):
            product = product + gram(train_ref, val_refs, layer, 0, group) * gram(
                train_ref, val_refs, layer, 1, group
            )
        sums.append(token_sums(product, tokens))
    return example_sums(jnp.concatenate(sums, axis=0), tokens)


def cut_kernel(val_ref, *part_refs):
    for c, ref in enumerate(part_refs, 1):
        depth = ref.shape[-1]
        ref[...] = val_ref[..., c * depth : (c + 1) * depth]


def first_cut_kernel(val_ref, part_ref, sems):
    copies = [
        pltpu.make_async_copy(val_ref.at[v, ..., : part_ref.shape[-1]], part_ref.at[v], sems.at[v])
        for v in range(part_ref.shape[0])
    ]
    for copy in copies:
        copy.start()
    for copy in copies:
        copy.wait()


def scores_kernel(train_ref, *refs):
    *val_refs, out_ref = refs
    out_ref[...] = scores(train_ref, val_refs)


def by_parity(even, odd):
    parity = lax.rem(lax.axis_index("blk"), 2)
    pl.when(parity == 0)(even)
    pl.when(parity == 1)(odd)


def pick_kernel(even_ref, odd_ref, *refs):
    out_ref = refs[-1]

    def put(ref):
        out_ref[...] = ref[...]

    by_parity(lambda: put(even_ref), lambda: put(odd_ref))


def pick_last_kernel(even_ref, odd_ref, *refs):
    out_ref = refs[-1]
    count = out_ref.shape[0]

    def put(ref):
        out_ref[...] = ref[ref.shape[0] - count :]

    by_parity(lambda: put(even_ref), lambda: put(odd_ref))


def columns(first, count, tokens):
    return slice(first * tokens, (first + count) * tokens)


def grams_kernel(train_ref, *refs):
    *part_refs, out_ref = refs
    layers, tokens = train_ref.shape[1], train_ref.shape[3]
    for layer in range(layers):
        for index in range(2):
            for group in groups(train_ref):
                rows = slice(group.start * tokens, group.stop * tokens)
                out_ref[layer, index, rows] = gram(train_ref, part_refs, layer, index, group)


def second_kernel(train_ref, part_ref, grams_ref, out_ref):
    layers, tokens, features = train_ref.shape[1], train_ref.shape[3], train_ref.shape[4]
    start = features - part_ref.shape[-1]
    sums = []
    for group in groups(train_ref):
        rows = slice(group.start * tokens, group.stop * tokens)
        product = 0.0
        for layer in range(layers):
            act, grad = (
                grams_ref[layer, index, rows] + gram(train_ref, [part_ref], layer, index, group, start)
                for index in range(2)
            )
            product = product + act * grad
        sums.append(token_sums(product, tokens))
    out_ref[...] = example_sums(jnp.concatenate(sums, axis=0), tokens)


def middle_kernel(train_ref, part_ref, last_ref, grams_ref, ends_ref, out_ref):
    layers, tokens, features = train_ref.shape[1], train_ref.shape[3], train_ref.shape[4]
    depth = part_ref.shape[-1]
    detour = columns(0, out_ref.shape[0], tokens)
    rest = slice(detour.stop, grams_ref.shape[-1])
    sums = []
    for group in groups(train_ref):
        rows = slice(group.start * tokens, group.stop * tokens)
        product = 0.0
        for layer in range(layers):
            totals = [
                grams_ref[layer, index, rows]
                + gram(train_ref, [part_ref], layer, index, group, features - 2 * depth)
                for index in range(2)
            ]
            act, grad = (
                totals[index][:, detour]
                + gram(train_ref, [last_ref], layer, index, group, features - depth)
                for index in range(2)
            )
            product = product + act * grad
            for index in range(2):
                ends_ref[layer, index, rows] = totals[index][:, rest]
        sums.append(token_sums(product, tokens))
    out_ref[...] = example_sums(jnp.concatenate(sums, axis=0), tokens)


def last_kernel(train_ref, end_ref, ends_ref, own_ref, first_ref, second_ref, out_ref):
    layers, tokens, features = train_ref.shape[1], train_ref.shape[3], train_ref.shape[4]
    start = features - end_ref.shape[-1]
    sums = []
    for group in groups(train_ref):
        rows = slice(group.start * tokens, group.stop * tokens)
        product = 0.0
        for layer in range(layers):
            act, grad = (
                ends_ref[layer, index, rows] + gram(train_ref, [end_ref], layer, index, group, start)
                for index in range(2)
            )
            product = product + act * grad
        sums.append(token_sums(product, tokens))
    ready = first_ref.shape[0]
    out_ref[0] = own_ref[...]
    out_ref[1, :ready] = first_ref[...]
    out_ref[1, ready:] = example_sums(jnp.concatenate(sums, axis=0), tokens)
    out_ref[2] = second_ref[...]


def sum_kernel(a_ref, b_ref, out_ref):
    out_ref[...] = a_ref[...] + b_ref[...]


def summed(rows, axis):
    if lax.axis_size(axis) != 2:
        return lax.psum(rows, axis)
    shape = jax.ShapeDtypeStruct(rows.shape, rows.dtype)
    return call(sum_kernel, shape, [VMEM] * 2, [rows, permuted(rows, axis, lambda i: i ^ 1)])


def local(train, val):
    examples, layers, _, tokens, features = train.shape
    count = val.shape[0]
    cuts = CUTS
    depth = features // cuts
    work = 4 * examples * count * layers * tokens * tokens * features
    part = jax.ShapeDtypeStruct(val.shape[:-1] + (depth,), val.dtype)
    small = jax.ShapeDtypeStruct((1,) + part.shape[1:], val.dtype)
    rows = jax.ShapeDtypeStruct((count, examples), jnp.float32)
    grams = jax.ShapeDtypeStruct((layers, 2, examples * tokens, count * tokens), jnp.float32)

    detour = val[: count - 1, ..., (cuts - 1) * depth :]
    sems = [pltpu.SemaphoreType.DMA((count,))]
    first_part = call(first_cut_kernel, part, [HBM], [val], scratch=sems, vmem=107 << 19)
    parts = [first_part, *call(cut_kernel, [part] * (cuts - 1), [VMEM], [val])]
    second = [permuted(x, "blk", lambda i: i + 2) for x in parts]
    near_last = permuted(detour, "blk", lambda i: i ^ 1)
    far_last = permuted(near_last, "blk", lambda i: i + 2)
    first = []
    for c in range(cuts - 1):
        operands = [parts[c], second[c]] + ([near_last] if c == 1 else [])
        picked = call(pick_kernel, part, [VMEM] * len(operands), operands)
        first.append(permuted(picked, "blk", lambda i: i ^ 1))
    sums = call(grams_kernel, grams, [VMEM] * (cuts - 1), [train] + first[:-1], work // 2)
    far = call(grams_kernel, grams, [VMEM] * cuts, [train] + second[:-1], work)
    operands = [parts[-1], second[-1], far]
    picked = call(pick_last_kernel, small, [VMEM] * len(operands), operands)
    end = permuted(picked, "blk", lambda i: i ^ 1)

    own = call(scores_kernel, rows, [VMEM] * (1 + cuts), [train] + parts, work)
    far = call(second_kernel, rows, [VMEM] * 3, [train, second[-1], far], work // 4)
    last = call(pick_kernel, detour, [VMEM] * 3, [far_last, near_last, sums], work)
    ends = jax.ShapeDtypeStruct(grams.shape[:-1] + (tokens,), jnp.float32)
    ready = jax.ShapeDtypeStruct((count - 1, examples), jnp.float32)
    operands = [train, first[-1], last, sums]
    ends, ready = call(middle_kernel, [ends, ready], [VMEM] * len(operands), operands, work // 4)
    out = jax.ShapeDtypeStruct((3,) + rows.shape, jnp.float32)
    operands = [train, end, ends, own, ready, far]
    partial_rows = call(last_kernel, out, [VMEM] * len(operands), operands, work // 16)
    return summed(partial_rows, "layer").transpose(2, 0, 1)


def solution(mesh):
    return jax.shard_map(
        local,
        mesh=mesh,
        in_specs=(P("blk", "layer", None, None, None), P("blk", "layer", None, None, None)),
        out_specs=P("blk", None, None),
        check_vma=False,
    )
```

```python
import functools

import jax
import jax.numpy as jnp
from jax import lax
from jax.experimental import pallas as pl
from jax.experimental.pallas import tpu as pltpu
from jax.sharding import PartitionSpec as P

CUTS = 4
GROUP = 4

VMEM = pl.BlockSpec(memory_space=pltpu.VMEM)


def permuted(block, axis, target):
    size = lax.axis_size(axis)
    return lax.ppermute(block, axis, [(i, target(i) % size) for i in range(size)])


def call(kernel, out_shape, specs, operands, flops=0, scratch=(), vmem=16 << 20):
    shapes = list(operands) + jax.tree.leaves(out_shape)
    return pl.pallas_call(
        kernel,
        out_shape=out_shape,
        in_specs=specs,
        out_specs=jax.tree.map(lambda _: VMEM, out_shape),
        scratch_shapes=scratch,
        compiler_params=pltpu.CompilerParams(vmem_limit_bytes=vmem),
        cost_estimate=pl.CostEstimate(
            flops=flops,
            bytes_accessed=sum(x.size * x.dtype.itemsize for x in shapes),
            transcendentals=0,
        ),
    )(*operands)


def groups(train_ref):
    examples = train_ref.shape[0]
    size = GROUP if examples % GROUP == 0 else 1
    return [slice(first, first + size) for first in range(0, examples, size)]


def gram(train_ref, val_refs, layer, index, group, start=0):
    total = 0.0
    for ref in val_refs:
        depth = ref.shape[-1]
        train = train_ref[group, layer, index, :, start : start + depth].reshape(-1, depth)
        val = ref[:, layer, index].reshape(-1, depth)
        total = total + lax.dot_general(
            train, val, (((1,), (1,)), ((), ())), preferred_element_type=jnp.float32
        )
        start += depth
    return total


def token_sums(product, tokens):
    return jnp.sum(product.reshape(-1, tokens, product.shape[-1]), axis=1)


def example_sums(by_token, tokens):
    count = by_token.shape[-1] // tokens
    shape = (count, by_token.shape[-1])
    token = lax.broadcasted_iota(jnp.int32, shape, 1) // tokens
    mine = (token == lax.broadcasted_iota(jnp.int32, shape, 0)).astype(jnp.bfloat16)
    total, rest = 0.0, by_token
    for _ in range(3):
        piece = rest.astype(jnp.bfloat16)
        rest = rest - piece.astype(jnp.float32)
        total = total + lax.dot_general(
            mine, piece, (((1,), (1,)), ((), ())), preferred_element_type=jnp.float32
        )
    return total


def scores(train_ref, val_refs):
    layers, tokens = train_ref.shape[1], train_ref.shape[3]
    sums = []
    for group in groups(train_ref):
        product = 0.0
        for layer in range(layers):
            product = product + gram(train_ref, val_refs, layer, 0, group) * gram(
                train_ref, val_refs, layer, 1, group
            )
        sums.append(token_sums(product, tokens))
    return example_sums(jnp.concatenate(sums, axis=0), tokens)


def cut_kernel(val_ref, *refs):
    *part_refs, joint_ref = refs
    for c, ref in enumerate(part_refs, 1):
        depth = ref.shape[-1]
        ref[...] = val_ref[..., c * depth : (c + 1) * depth]
    count = val_ref.shape[0]
    joint_ref[:count] = part_refs[-2][...]
    joint_ref[count:] = part_refs[-1][count - 1 :]


def scores_kernel(train_ref, *refs):
    *val_refs, out_ref = refs
    out_ref[...] = scores(train_ref, val_refs)


def by_parity(even, odd):
    parity = lax.rem(lax.axis_index("blk"), 2)
    pl.when(parity == 0)(even)
    pl.when(parity == 1)(odd)


def pick_kernel(even_ref, odd_ref, *refs):
    out_ref = refs[-1]

    def put(ref):
        out_ref[...] = ref[...]

    by_parity(lambda: put(even_ref), lambda: put(odd_ref))


def pick_joint_kernel(even_ref, odd_ref, out_ref, end_ref):
    count = out_ref.shape[0]

    def put(ref):
        out_ref[...] = ref[:count]
        end_ref[...] = ref[count:]

    by_parity(lambda: put(even_ref), lambda: put(odd_ref))


def columns(first, count, tokens):
    return slice(first * tokens, (first + count) * tokens)


def grams_kernel(train_ref, *refs):
    *part_refs, out_ref = refs
    layers, tokens = train_ref.shape[1], train_ref.shape[3]
    for layer in range(layers):
        for index in range(2):
            for group in groups(train_ref):
                rows = slice(group.start * tokens, group.stop * tokens)
                out_ref[layer, index, rows] = gram(train_ref, part_refs, layer, index, group)


def far_kernel(train_ref, *refs):
    *part_refs, joint_ref, out_ref = refs
    grams_kernel(train_ref, *part_refs, joint_ref.at[: part_refs[0].shape[0]], out_ref)


def second_kernel(train_ref, detour_ref, joint_ref, grams_ref, out_ref):
    layers, tokens, features = train_ref.shape[1], train_ref.shape[3], train_ref.shape[4]
    start, split, count = features - detour_ref.shape[-1], detour_ref.shape[0], out_ref.shape[0]
    for first, stop, ref in ((0, split, detour_ref), (split, count, joint_ref.at[count:])):
        cols = columns(first, stop - first, tokens)
        sums = []
        for group in groups(train_ref):
            rows = slice(group.start * tokens, group.stop * tokens)
            product = 0.0
            for layer in range(layers):
                act, grad = (
                    grams_ref[layer, index, rows, cols] + gram(train_ref, [ref], layer, index, group, start)
                    for index in range(2)
                )
                product = product + act * grad
            sums.append(token_sums(product, tokens))
        out_ref[first:stop] = example_sums(jnp.concatenate(sums, axis=0), tokens)


def middle_kernel(train_ref, part_ref, last_ref, grams_ref, ends_ref, out_ref):
    layers, tokens, features = train_ref.shape[1], train_ref.shape[3], train_ref.shape[4]
    depth = part_ref.shape[-1]
    detour = columns(0, out_ref.shape[0], tokens)
    rest = slice(detour.stop, grams_ref.shape[-1])
    sums = []
    for group in groups(train_ref):
        rows = slice(group.start * tokens, group.stop * tokens)
        product = 0.0
        for layer in range(layers):
            totals = [
                grams_ref[layer, index, rows]
                + gram(train_ref, [part_ref], layer, index, group, features - 2 * depth)
                for index in range(2)
            ]
            act, grad = (
                totals[index][:, detour]
                + gram(train_ref, [last_ref], layer, index, group, features - depth)
                for index in range(2)
            )
            product = product + act * grad
            for index in range(2):
                ends_ref[layer, index, rows] = totals[index][:, rest]
        sums.append(token_sums(product, tokens))
    out_ref[...] = example_sums(jnp.concatenate(sums, axis=0), tokens)


def last_kernel(train_ref, end_ref, ends_ref, own_ref, first_ref, second_ref, out_ref):
    layers, tokens, features = train_ref.shape[1], train_ref.shape[3], train_ref.shape[4]
    start = features - end_ref.shape[-1]
    sums = []
    for group in groups(train_ref):
        rows = slice(group.start * tokens, group.stop * tokens)
        product = 0.0
        for layer in range(layers):
            act, grad = (
                ends_ref[layer, index, rows] + gram(train_ref, [end_ref], layer, index, group, start)
                for index in range(2)
            )
            product = product + act * grad
        sums.append(token_sums(product, tokens))
    ready = first_ref.shape[0]
    out_ref[0] = own_ref[...]
    out_ref[1, :ready] = first_ref[...]
    out_ref[1, ready:] = example_sums(jnp.concatenate(sums, axis=0), tokens)
    out_ref[2] = second_ref[...]


def summed(rows, axis):
    if lax.axis_size(axis) != 2:
        return lax.psum(rows, axis)
    return rows + permuted(rows, axis, lambda i: i ^ 1)


def local(train, val):
    examples, layers, _, tokens, features = train.shape
    count = val.shape[0]
    cuts = CUTS
    depth = features // cuts
    work = 4 * examples * count * layers * tokens * tokens * features
    part = jax.ShapeDtypeStruct(val.shape[:-1] + (depth,), val.dtype)
    small = jax.ShapeDtypeStruct((1,) + part.shape[1:], val.dtype)
    rows = jax.ShapeDtypeStruct((count, examples), jnp.float32)
    grams = jax.ShapeDtypeStruct((layers, 2, examples * tokens, count * tokens), jnp.float32)

    detour = val[: count - 1, ..., (cuts - 1) * depth :]
    joint = jax.ShapeDtypeStruct((count + 1,) + part.shape[1:], val.dtype)
    *parts, joint = call(cut_kernel, [part] * (cuts - 1) + [joint], [VMEM], [val])
    parts = [val[..., :depth]] + parts
    second = [permuted(x, "blk", lambda i: i + 2) for x in parts[:-2] + [joint]]
    near_last = permuted(detour, "blk", lambda i: i ^ 1)
    second_detour = permuted(detour, "blk", lambda i: i + 2)
    far_last = permuted(near_last, "blk", lambda i: i + 2)
    first = []
    for c in range(cuts - 2):
        operands = [parts[c], second[c]] + ([near_last] if c == 1 else [])
        picked = call(pick_kernel, part, [VMEM] * len(operands), operands)
        first.append(permuted(picked, "blk", lambda i: i ^ 1))
    picked = call(pick_joint_kernel, [part, small], [VMEM] * 2, [joint, second[-1]])
    *first, end = first + [permuted(x, "blk", lambda i: i ^ 1) for x in picked]
    sums = call(grams_kernel, grams, [VMEM] * (cuts - 1), [train] + first[:-1], work // 2)
    far = call(far_kernel, grams, [VMEM] * cuts, [train] + second, work)

    own = call(scores_kernel, rows, [VMEM] * (1 + cuts), [train] + parts, work)
    operands = [train, second_detour, second[-1], far]
    far = call(second_kernel, rows, [VMEM] * len(operands), operands, work // 4)
    last = call(pick_kernel, detour, [VMEM] * 3, [far_last, near_last, sums], work)
    ends = jax.ShapeDtypeStruct(grams.shape[:-1] + (tokens,), jnp.float32)
    ready = jax.ShapeDtypeStruct((count - 1, examples), jnp.float32)
    operands = [train, first[-1], last, sums]
    ends, ready = call(middle_kernel, [ends, ready], [VMEM] * len(operands), operands, work // 4)
    out = jax.ShapeDtypeStruct((3,) + rows.shape, jnp.float32)
    operands = [train, end, ends, own, ready, far]
    partial_rows = call(last_kernel, out, [VMEM] * len(operands), operands, work // 16)
    return summed(partial_rows, "layer").transpose(2, 0, 1)


def solution(mesh):
    return jax.shard_map(
        local,
        mesh=mesh,
        in_specs=(P("blk", "layer", None, None, None), P("blk", "layer", None, None, None)),
        out_specs=P("blk", None, None),
        check_vma=False,
    )
```

```python
import functools

import jax
import jax.numpy as jnp
from jax import lax
from jax.experimental import pallas as pl
from jax.experimental.pallas import tpu as pltpu
from jax.sharding import PartitionSpec as P

CUTS = 4
GROUP = 4

VMEM = pl.BlockSpec(memory_space=pltpu.VMEM)


def permuted(block, axis, target):
    size = lax.axis_size(axis)
    return lax.ppermute(block, axis, [(i, target(i) % size) for i in range(size)])


def call(kernel, out_shape, specs, operands, flops=0, scratch=(), vmem=16 << 20):
    shapes = list(operands) + jax.tree.leaves(out_shape)
    return pl.pallas_call(
        kernel,
        out_shape=out_shape,
        in_specs=specs,
        out_specs=jax.tree.map(lambda _: VMEM, out_shape),
        scratch_shapes=scratch,
        compiler_params=pltpu.CompilerParams(vmem_limit_bytes=vmem),
        cost_estimate=pl.CostEstimate(
            flops=flops,
            bytes_accessed=sum(x.size * x.dtype.itemsize for x in shapes),
            transcendentals=0,
        ),
    )(*operands)


def groups(train_ref):
    examples = train_ref.shape[0]
    size = GROUP if examples % GROUP == 0 else 1
    return [slice(first, first + size) for first in range(0, examples, size)]


def gram(train_ref, val_refs, layer, index, group, start=0):
    total = 0.0
    for ref in val_refs:
        depth = ref.shape[-1]
        train = train_ref[group, layer, index, :, start : start + depth].reshape(-1, depth)
        val = ref[:, layer, index].reshape(-1, depth)
        total = total + lax.dot_general(
            train, val, (((1,), (1,)), ((), ())), preferred_element_type=jnp.float32
        )
        start += depth
    return total


def token_sums(product, tokens):
    return jnp.sum(product.reshape(-1, tokens, product.shape[-1]), axis=1)


def example_sums(by_token, tokens):
    count = by_token.shape[-1] // tokens
    shape = (count, by_token.shape[-1])
    token = lax.broadcasted_iota(jnp.int32, shape, 1) // tokens
    mine = (token == lax.broadcasted_iota(jnp.int32, shape, 0)).astype(jnp.bfloat16)
    total, rest = 0.0, by_token
    for _ in range(3):
        piece = rest.astype(jnp.bfloat16)
        rest = rest - piece.astype(jnp.float32)
        total = total + lax.dot_general(
            mine, piece, (((1,), (1,)), ((), ())), preferred_element_type=jnp.float32
        )
    return total


def scores(train_ref, val_refs):
    layers, tokens = train_ref.shape[1], train_ref.shape[3]
    sums = []
    for group in groups(train_ref):
        product = 0.0
        for layer in range(layers):
            product = product + gram(train_ref, val_refs, layer, 0, group) * gram(
                train_ref, val_refs, layer, 1, group
            )
        sums.append(token_sums(product, tokens))
    return example_sums(jnp.concatenate(sums, axis=0), tokens)


def cut_kernel(val_ref, *refs):
    *part_refs, joint_ref = refs
    for c, ref in enumerate(part_refs, 1):
        depth = ref.shape[-1]
        ref[...] = val_ref[..., c * depth : (c + 1) * depth]
    count = val_ref.shape[0]
    joint_ref[:count] = part_refs[-2][...]
    joint_ref[count:] = part_refs[-1][count - 1 :]


def scores_kernel(train_ref, *refs):
    *val_refs, out_ref = refs
    out_ref[...] = scores(train_ref, val_refs)


def by_parity(even, odd):
    parity = lax.rem(lax.axis_index("blk"), 2)
    pl.when(parity == 0)(even)
    pl.when(parity == 1)(odd)


def pick_kernel(even_ref, odd_ref, *refs):
    out_ref = refs[-1]

    def put(ref):
        out_ref[...] = ref[...]

    by_parity(lambda: put(even_ref), lambda: put(odd_ref))


def columns(first, count, tokens):
    return slice(first * tokens, (first + count) * tokens)


def grams_kernel(train_ref, *refs):
    *part_refs, out_ref = refs
    layers, tokens = train_ref.shape[1], train_ref.shape[3]
    for layer in range(layers):
        for index in range(2):
            for group in groups(train_ref):
                rows = slice(group.start * tokens, group.stop * tokens)
                out_ref[layer, index, rows] = gram(train_ref, part_refs, layer, index, group)


def far_kernel(train_ref, *refs):
    *part_refs, joint_ref, out_ref = refs
    grams_kernel(train_ref, *part_refs, joint_ref.at[: part_refs[0].shape[0]], out_ref)


def second_kernel(train_ref, detour_ref, joint_ref, grams_ref, out_ref):
    layers, tokens, features = train_ref.shape[1], train_ref.shape[3], train_ref.shape[4]
    start, split, count = features - detour_ref.shape[-1], detour_ref.shape[0], out_ref.shape[0]
    for first, stop, ref in ((0, split, detour_ref), (split, count, joint_ref.at[count:])):
        cols = columns(first, stop - first, tokens)
        sums = []
        for group in groups(train_ref):
            rows = slice(group.start * tokens, group.stop * tokens)
            product = 0.0
            for layer in range(layers):
                act, grad = (
                    grams_ref[layer, index, rows, cols] + gram(train_ref, [ref], layer, index, group, start)
                    for index in range(2)
                )
                product = product + act * grad
            sums.append(token_sums(product, tokens))
        out_ref[first:stop] = example_sums(jnp.concatenate(sums, axis=0), tokens)


def last_kernel(train_ref, joint_ref, last_ref, grams_ref, own_ref, second_ref, out_ref):
    layers, tokens, features = train_ref.shape[1], train_ref.shape[3], train_ref.shape[4]
    depth, split, count = joint_ref.shape[-1], last_ref.shape[0], out_ref.shape[1]
    refs = (last_ref, joint_ref.at[count:])
    cols = (columns(0, split, tokens), columns(split, count - split, tokens))
    sums = ([], [])
    for group in groups(train_ref):
        rows = slice(group.start * tokens, group.stop * tokens)
        products = [0.0, 0.0]
        for layer in range(layers):
            totals = [
                grams_ref[layer, index, rows]
                + gram(train_ref, [joint_ref.at[:count]], layer, index, group, features - 2 * depth)
                for index in range(2)
            ]
            for n in range(2):
                act, grad = (
                    totals[index][:, cols[n]]
                    + gram(train_ref, [refs[n]], layer, index, group, features - depth)
                    for index in range(2)
                )
                products[n] = products[n] + act * grad
        for n in range(2):
            sums[n].append(token_sums(products[n], tokens))
    out_ref[0] = own_ref[...]
    out_ref[1, :split] = example_sums(jnp.concatenate(sums[0], axis=0), tokens)
    out_ref[1, split:] = example_sums(jnp.concatenate(sums[1], axis=0), tokens)
    out_ref[2] = second_ref[...]


def summed(rows, axis):
    if lax.axis_size(axis) != 2:
        return lax.psum(rows, axis)
    return rows + permuted(rows, axis, lambda i: i ^ 1)


def local(train, val):
    examples, layers, _, tokens, features = train.shape
    count = val.shape[0]
    cuts = CUTS
    depth = features // cuts
    work = 4 * examples * count * layers * tokens * tokens * features
    part = jax.ShapeDtypeStruct(val.shape[:-1] + (depth,), val.dtype)
    rows = jax.ShapeDtypeStruct((count, examples), jnp.float32)
    grams = jax.ShapeDtypeStruct((layers, 2, examples * tokens, count * tokens), jnp.float32)

    detour = val[: count - 1, ..., (cuts - 1) * depth :]
    joint = jax.ShapeDtypeStruct((count + 1,) + part.shape[1:], val.dtype)
    *parts, joint = call(cut_kernel, [part] * (cuts - 1) + [joint], [VMEM], [val])
    parts = [val[..., :depth]] + parts
    second = [permuted(x, "blk", lambda i: i + 2) for x in parts[:-2] + [joint]]
    near_last = permuted(detour, "blk", lambda i: i ^ 1)
    second_detour = permuted(detour, "blk", lambda i: i + 2)
    far_last = permuted(near_last, "blk", lambda i: i + 2)
    first = []
    for c in range(cuts - 2):
        operands = [parts[c], second[c]] + ([near_last] if c == 1 else [])
        picked = call(pick_kernel, part, [VMEM] * len(operands), operands)
        first.append(permuted(picked, "blk", lambda i: i ^ 1))
    shape = jax.ShapeDtypeStruct(joint.shape, joint.dtype)
    picked = call(pick_kernel, shape, [VMEM] * 2, [joint, second[-1]])
    first.append(permuted(picked, "blk", lambda i: i ^ 1))
    sums = call(grams_kernel, grams, [VMEM] * (cuts - 1), [train] + first[:-1], work // 2)
    far = call(far_kernel, grams, [VMEM] * cuts, [train] + second, work)

    own = call(scores_kernel, rows, [VMEM] * (1 + cuts), [train] + parts, work)
    operands = [train, second_detour, second[-1], far]
    far = call(second_kernel, rows, [VMEM] * len(operands), operands, work // 4)
    last = call(pick_kernel, detour, [VMEM] * 3, [far_last, near_last, sums], 2 * work)
    out = jax.ShapeDtypeStruct((3,) + rows.shape, jnp.float32)
    operands = [train, first[-1], last, sums, own, far]
    partial_rows = call(last_kernel, out, [VMEM] * len(operands), operands, work // 4)
    return summed(partial_rows, "layer").transpose(2, 0, 1)


def solution(mesh):
    return jax.shard_map(
        local,
        mesh=mesh,
        in_specs=(P("blk", "layer", None, None, None), P("blk", "layer", None, None, None)),
        out_specs=P("blk", None, None),
        check_vma=False,
    )
```

```python
import functools

import jax
import jax.numpy as jnp
from jax import lax
from jax.experimental import pallas as pl
from jax.experimental.pallas import tpu as pltpu
from jax.sharding import PartitionSpec as P

CUTS = 4
GROUP = 4

VMEM = pl.BlockSpec(memory_space=pltpu.VMEM)


def permuted(block, axis, target):
    size = lax.axis_size(axis)
    return lax.ppermute(block, axis, [(i, target(i) % size) for i in range(size)])


def call(kernel, out_shape, specs, operands, flops=0, scratch=(), vmem=16 << 20):
    shapes = list(operands) + jax.tree.leaves(out_shape)
    return pl.pallas_call(
        kernel,
        out_shape=out_shape,
        in_specs=specs,
        out_specs=jax.tree.map(lambda _: VMEM, out_shape),
        scratch_shapes=scratch,
        compiler_params=pltpu.CompilerParams(vmem_limit_bytes=vmem),
        cost_estimate=pl.CostEstimate(
            flops=flops,
            bytes_accessed=sum(x.size * x.dtype.itemsize for x in shapes),
            transcendentals=0,
        ),
    )(*operands)


def groups(train_ref):
    examples = train_ref.shape[0]
    size = GROUP if examples % GROUP == 0 else 1
    return [slice(first, first + size) for first in range(0, examples, size)]


def gram(train_ref, val_refs, layer, index, group, start=0):
    total = 0.0
    for ref in val_refs:
        depth = ref.shape[-1]
        train = train_ref[group, layer, index, :, start : start + depth].reshape(-1, depth)
        val = ref[:, layer, index].reshape(-1, depth)
        total = total + lax.dot_general(
            train, val, (((1,), (1,)), ((), ())), preferred_element_type=jnp.float32
        )
        start += depth
    return total


def token_sums(product, tokens):
    return jnp.sum(product.reshape(-1, tokens, product.shape[-1]), axis=1)


def example_sums(by_token, tokens):
    count = by_token.shape[-1] // tokens
    shape = (count, by_token.shape[-1])
    token = lax.broadcasted_iota(jnp.int32, shape, 1) // tokens
    mine = (token == lax.broadcasted_iota(jnp.int32, shape, 0)).astype(jnp.bfloat16)
    total, rest = 0.0, by_token
    for _ in range(3):
        piece = rest.astype(jnp.bfloat16)
        rest = rest - piece.astype(jnp.float32)
        total = total + lax.dot_general(
            mine, piece, (((1,), (1,)), ((), ())), preferred_element_type=jnp.float32
        )
    return total


def scores(train_ref, val_refs):
    layers, tokens = train_ref.shape[1], train_ref.shape[3]
    sums = []
    for group in groups(train_ref):
        product = 0.0
        for layer in range(layers):
            product = product + gram(train_ref, val_refs, layer, 0, group) * gram(
                train_ref, val_refs, layer, 1, group
            )
        sums.append(token_sums(product, tokens))
    return example_sums(jnp.concatenate(sums, axis=0), tokens)


def cut_kernel(val_ref, *refs):
    *part_refs, joint_ref = refs
    for c, ref in enumerate(part_refs, 1):
        depth = ref.shape[-1]
        ref[...] = val_ref[..., c * depth : (c + 1) * depth]
    count = val_ref.shape[0]
    joint_ref[:count] = part_refs[-2][...]
    joint_ref[count:] = part_refs[-1][count - 1 :]


def scores_kernel(train_ref, *refs):
    *val_refs, out_ref = refs
    out_ref[...] = scores(train_ref, val_refs)


def by_parity(even, odd):
    parity = lax.rem(lax.axis_index("blk"), 2)
    pl.when(parity == 0)(even)
    pl.when(parity == 1)(odd)


def pick_kernel(even_ref, odd_ref, *refs):
    out_ref = refs[-1]

    def put(ref):
        out_ref[...] = ref[...]

    by_parity(lambda: put(even_ref), lambda: put(odd_ref))


def columns(first, count, tokens):
    return slice(first * tokens, (first + count) * tokens)


def grams_kernel(train_ref, *refs):
    *part_refs, out_ref = refs
    layers, tokens = train_ref.shape[1], train_ref.shape[3]
    for layer in range(layers):
        for index in range(2):
            for group in groups(train_ref):
                rows = slice(group.start * tokens, group.stop * tokens)
                out_ref[layer, index, rows] = gram(train_ref, part_refs, layer, index, group)


def far_kernel(train_ref, *refs):
    *part_refs, joint_ref, out_ref = refs
    grams_kernel(train_ref, *part_refs, joint_ref.at[: part_refs[0].shape[0]], out_ref)


def second_kernel(train_ref, detour_ref, joint_ref, grams_ref, out_ref):
    layers, tokens, features = train_ref.shape[1], train_ref.shape[3], train_ref.shape[4]
    start, split, count = features - detour_ref.shape[-1], detour_ref.shape[0], out_ref.shape[0]
    for first, stop, ref in ((0, split, detour_ref), (split, count, joint_ref.at[count:])):
        cols = columns(first, stop - first, tokens)
        sums = []
        for group in groups(train_ref):
            rows = slice(group.start * tokens, group.stop * tokens)
            product = 0.0
            for layer in range(layers):
                act, grad = (
                    grams_ref[layer, index, rows, cols] + gram(train_ref, [ref], layer, index, group, start)
                    for index in range(2)
                )
                product = product + act * grad
            sums.append(token_sums(product, tokens))
        out_ref[first:stop] = example_sums(jnp.concatenate(sums, axis=0), tokens)


def add_kernel(train_ref, far_ref, near_ref, grams_ref, out_ref):
    layers, tokens, features = train_ref.shape[1], train_ref.shape[3], train_ref.shape[4]
    detour = columns(0, far_ref.shape[0], tokens)
    rest = slice(detour.stop, grams_ref.shape[-1])

    def add(last_ref):
        begin = features - last_ref.shape[-1]
        for layer in range(layers):
            for index in range(2):
                for group in groups(train_ref):
                    rows = slice(group.start * tokens, group.stop * tokens)
                    out_ref[layer, index, rows, detour] = grams_ref[layer, index, rows, detour] + gram(
                        train_ref, [last_ref], layer, index, group, begin
                    )

    out_ref[..., rest] = grams_ref[..., rest]
    by_parity(lambda: add(far_ref), lambda: add(near_ref))


def last_kernel(train_ref, joint_ref, grams_ref, own_ref, second_ref, out_ref):
    layers, tokens, features = train_ref.shape[1], train_ref.shape[3], train_ref.shape[4]
    depth, count = joint_ref.shape[-1], out_ref.shape[1]
    split = 2 * count - joint_ref.shape[0]
    cols = (columns(0, split, tokens), columns(split, count - split, tokens))
    sums = ([], [])
    for group in groups(train_ref):
        rows = slice(group.start * tokens, group.stop * tokens)
        products = [0.0, 0.0]
        for layer in range(layers):
            totals = [
                grams_ref[layer, index, rows]
                + gram(train_ref, [joint_ref.at[:count]], layer, index, group, features - 2 * depth)
                for index in range(2)
            ]
            for n in range(2):
                act, grad = (total[:, cols[n]] for total in totals)
                if n == 1:
                    ends = [
                        gram(train_ref, [joint_ref.at[count:]], layer, index, group, features - depth)
                        for index in range(2)
                    ]
                    act, grad = act + ends[0], grad + ends[1]
                products[n] = products[n] + act * grad
        for n in range(2):
            sums[n].append(token_sums(products[n], tokens))
    out_ref[0] = own_ref[...]
    out_ref[1, :split] = example_sums(jnp.concatenate(sums[0], axis=0), tokens)
    out_ref[1, split:] = example_sums(jnp.concatenate(sums[1], axis=0), tokens)
    out_ref[2] = second_ref[...]


def summed(rows, axis):
    if lax.axis_size(axis) != 2:
        return lax.psum(rows, axis)
    return rows + permuted(rows, axis, lambda i: i ^ 1)


def local(train, val):
    examples, layers, _, tokens, features = train.shape
    count = val.shape[0]
    cuts = CUTS
    depth = features // cuts
    work = 4 * examples * count * layers * tokens * tokens * features
    part = jax.ShapeDtypeStruct(val.shape[:-1] + (depth,), val.dtype)
    rows = jax.ShapeDtypeStruct((count, examples), jnp.float32)
    grams = jax.ShapeDtypeStruct((layers, 2, examples * tokens, count * tokens), jnp.float32)

    detour = val[: count - 1, ..., (cuts - 1) * depth :]
    joint = jax.ShapeDtypeStruct((count + 1,) + part.shape[1:], val.dtype)
    *parts, joint = call(cut_kernel, [part] * (cuts - 1) + [joint], [VMEM], [val])
    parts = [val[..., :depth]] + parts
    second = [permuted(x, "blk", lambda i: i + 2) for x in parts[:-2] + [joint]]
    near_last = permuted(detour, "blk", lambda i: i ^ 1)
    second_detour = permuted(detour, "blk", lambda i: i + 2)
    far_last = permuted(near_last, "blk", lambda i: i + 2)
    first = []
    for c in range(cuts - 2):
        operands = [parts[c], second[c]] + ([near_last] if c == 1 else [])
        picked = call(pick_kernel, part, [VMEM] * len(operands), operands)
        first.append(permuted(picked, "blk", lambda i: i ^ 1))
    shape = jax.ShapeDtypeStruct(joint.shape, joint.dtype)
    picked = call(pick_kernel, shape, [VMEM] * 2, [joint, second[-1]])
    first.append(permuted(picked, "blk", lambda i: i ^ 1))
    sums = call(grams_kernel, grams, [VMEM] * (cuts - 1), [train] + first[:-1], work // 2)
    far = call(far_kernel, grams, [VMEM] * cuts, [train] + second, work)

    own = call(scores_kernel, rows, [VMEM] * (1 + cuts), [train] + parts, work)
    operands = [train, second_detour, second[-1], far]
    far = call(second_kernel, rows, [VMEM] * len(operands), operands, work // 4)
    sums = call(add_kernel, grams, [VMEM] * 4, [train, far_last, near_last, sums], 2 * work)
    out = jax.ShapeDtypeStruct((3,) + rows.shape, jnp.float32)
    operands = [train, first[-1], sums, own, far]
    partial_rows = call(last_kernel, out, [VMEM] * len(operands), operands, work // 4)
    return summed(partial_rows, "layer").transpose(2, 0, 1)


def solution(mesh):
    return jax.shard_map(
        local,
        mesh=mesh,
        in_specs=(P("blk", "layer", None, None, None), P("blk", "layer", None, None, None)),
        out_specs=P("blk", None, None),
        check_vma=False,
    )
```

```python
import functools

import jax
import jax.numpy as jnp
from jax import lax
from jax.experimental import pallas as pl
from jax.experimental.pallas import tpu as pltpu
from jax.sharding import PartitionSpec as P

CUTS = 4
GROUP = 12

VMEM = pl.BlockSpec(memory_space=pltpu.VMEM)


def permuted(block, axis, target):
    size = lax.axis_size(axis)
    return lax.ppermute(block, axis, [(i, target(i) % size) for i in range(size)])


def call(kernel, out_shape, specs, operands, flops=0, scratch=(), vmem=16 << 20):
    shapes = list(operands) + jax.tree.leaves(out_shape)
    return pl.pallas_call(
        kernel,
        out_shape=out_shape,
        in_specs=specs,
        out_specs=jax.tree.map(lambda _: VMEM, out_shape),
        scratch_shapes=scratch,
        compiler_params=pltpu.CompilerParams(vmem_limit_bytes=vmem),
        cost_estimate=pl.CostEstimate(
            flops=flops,
            bytes_accessed=sum(x.size * x.dtype.itemsize for x in shapes),
            transcendentals=0,
        ),
    )(*operands)


def groups(train_ref):
    examples = train_ref.shape[0]
    size = GROUP if examples % GROUP == 0 else 1
    return [slice(first, first + size) for first in range(0, examples, size)]


def gram(train_ref, val_refs, layer, index, group, start=0):
    total = 0.0
    for ref in val_refs:
        depth = ref.shape[-1]
        train = train_ref[group, layer, index, :, start : start + depth].reshape(-1, depth)
        val = ref[:, layer, index].reshape(-1, depth)
        total = total + lax.dot_general(
            train, val, (((1,), (1,)), ((), ())), preferred_element_type=jnp.float32
        )
        start += depth
    return total


def token_sums(product, tokens):
    return jnp.sum(product.reshape(-1, tokens, product.shape[-1]), axis=1)


def example_sums(by_token, tokens):
    count = by_token.shape[-1] // tokens
    shape = (count, by_token.shape[-1])
    token = lax.broadcasted_iota(jnp.int32, shape, 1) // tokens
    mine = (token == lax.broadcasted_iota(jnp.int32, shape, 0)).astype(jnp.bfloat16)
    total, rest = 0.0, by_token
    for _ in range(3):
        piece = rest.astype(jnp.bfloat16)
        rest = rest - piece.astype(jnp.float32)
        total = total + lax.dot_general(
            mine, piece, (((1,), (1,)), ((), ())), preferred_element_type=jnp.float32
        )
    return total


def scores(train_ref, val_refs):
    layers, tokens = train_ref.shape[1], train_ref.shape[3]
    sums = []
    for group in groups(train_ref):
        product = 0.0
        for layer in range(layers):
            product = product + gram(train_ref, val_refs, layer, 0, group) * gram(
                train_ref, val_refs, layer, 1, group
            )
        sums.append(token_sums(product, tokens))
    return example_sums(jnp.concatenate(sums, axis=0), tokens)


def cut_kernel(val_ref, *refs):
    *part_refs, joint_ref = refs
    for c, ref in enumerate(part_refs, 1):
        depth = ref.shape[-1]
        ref[...] = val_ref[..., c * depth : (c + 1) * depth]
    count = val_ref.shape[0]
    joint_ref[:count] = part_refs[-2][...]
    joint_ref[count:] = part_refs[-1][count - 1 :]


def scores_kernel(train_ref, *refs):
    *val_refs, out_ref = refs
    out_ref[...] = scores(train_ref, val_refs)


def by_parity(even, odd):
    parity = lax.rem(lax.axis_index("blk"), 2)
    pl.when(parity == 0)(even)
    pl.when(parity == 1)(odd)


def pick_kernel(even_ref, odd_ref, *refs):
    out_ref = refs[-1]

    def put(ref):
        out_ref[...] = ref[...]

    by_parity(lambda: put(even_ref), lambda: put(odd_ref))


def columns(first, count, tokens):
    return slice(first * tokens, (first + count) * tokens)


def grams_kernel(train_ref, *refs):
    *part_refs, out_ref = refs
    layers, tokens = train_ref.shape[1], train_ref.shape[3]
    for layer in range(layers):
        for index in range(2):
            for group in groups(train_ref):
                rows = slice(group.start * tokens, group.stop * tokens)
                out_ref[layer, index, rows] = gram(train_ref, part_refs, layer, index, group)


def far_kernel(train_ref, *refs):
    *part_refs, joint_ref, out_ref = refs
    grams_kernel(train_ref, *part_refs, joint_ref.at[: part_refs[0].shape[0]], out_ref)


def second_kernel(train_ref, detour_ref, joint_ref, grams_ref, out_ref):
    layers, tokens, features = train_ref.shape[1], train_ref.shape[3], train_ref.shape[4]
    start, split, count = features - detour_ref.shape[-1], detour_ref.shape[0], out_ref.shape[0]
    for first, stop, ref in ((0, split, detour_ref), (split, count, joint_ref.at[count:])):
        cols = columns(first, stop - first, tokens)
        sums = []
        for group in groups(train_ref):
            rows = slice(group.start * tokens, group.stop * tokens)
            product = 0.0
            for layer in range(layers):
                act, grad = (
                    grams_ref[layer, index, rows, cols] + gram(train_ref, [ref], layer, index, group, start)
                    for index in range(2)
                )
                product = product + act * grad
            sums.append(token_sums(product, tokens))
        out_ref[first:stop] = example_sums(jnp.concatenate(sums, axis=0), tokens)


def add_kernel(train_ref, far_ref, near_ref, grams_ref, out_ref):
    layers, tokens, features = train_ref.shape[1], train_ref.shape[3], train_ref.shape[4]
    detour = columns(0, far_ref.shape[0], tokens)
    rest = slice(detour.stop, grams_ref.shape[-1])

    def add(last_ref):
        begin = features - last_ref.shape[-1]
        for layer in range(layers):
            for index in range(2):
                for group in groups(train_ref):
                    rows = slice(group.start * tokens, group.stop * tokens)
                    out_ref[layer, index, rows, detour] = grams_ref[layer, index, rows, detour] + gram(
                        train_ref, [last_ref], layer, index, group, begin
                    )

    out_ref[..., rest] = grams_ref[..., rest]
    by_parity(lambda: add(far_ref), lambda: add(near_ref))


def last_kernel(train_ref, joint_ref, grams_ref, own_ref, second_ref, out_ref):
    layers, tokens, features = train_ref.shape[1], train_ref.shape[3], train_ref.shape[4]
    depth, count = joint_ref.shape[-1], out_ref.shape[1]
    split = 2 * count - joint_ref.shape[0]
    cols = (columns(0, split, tokens), columns(split, count - split, tokens))
    sums = ([], [])
    for group in groups(train_ref):
        rows = slice(group.start * tokens, group.stop * tokens)
        products = [0.0, 0.0]
        for layer in range(layers):
            totals = [
                grams_ref[layer, index, rows]
                + gram(train_ref, [joint_ref.at[:count]], layer, index, group, features - 2 * depth)
                for index in range(2)
            ]
            for n in range(2):
                act, grad = (total[:, cols[n]] for total in totals)
                if n == 1:
                    ends = [
                        gram(train_ref, [joint_ref.at[count:]], layer, index, group, features - depth)
                        for index in range(2)
                    ]
                    act, grad = act + ends[0], grad + ends[1]
                products[n] = products[n] + act * grad
        for n in range(2):
            sums[n].append(token_sums(products[n], tokens))
    out_ref[0] = own_ref[...]
    out_ref[1, :split] = example_sums(jnp.concatenate(sums[0], axis=0), tokens)
    out_ref[1, split:] = example_sums(jnp.concatenate(sums[1], axis=0), tokens)
    out_ref[2] = second_ref[...]


def summed(rows, axis):
    if lax.axis_size(axis) != 2:
        return lax.psum(rows, axis)
    return rows + permuted(rows, axis, lambda i: i ^ 1)


def local(train, val):
    examples, layers, _, tokens, features = train.shape
    count = val.shape[0]
    cuts = CUTS
    depth = features // cuts
    work = 4 * examples * count * layers * tokens * tokens * features
    part = jax.ShapeDtypeStruct(val.shape[:-1] + (depth,), val.dtype)
    rows = jax.ShapeDtypeStruct((count, examples), jnp.float32)
    grams = jax.ShapeDtypeStruct((layers, 2, examples * tokens, count * tokens), jnp.float32)

    detour = val[: count - 1, ..., (cuts - 1) * depth :]
    joint = jax.ShapeDtypeStruct((count + 1,) + part.shape[1:], val.dtype)
    *parts, joint = call(cut_kernel, [part] * (cuts - 1) + [joint], [VMEM], [val])
    parts = [val[..., :depth]] + parts
    second = [permuted(x, "blk", lambda i: i + 2) for x in parts[:-2] + [joint]]
    near_last = permuted(detour, "blk", lambda i: i ^ 1)
    second_detour = permuted(detour, "blk", lambda i: i + 2)
    far_last = permuted(near_last, "blk", lambda i: i + 2)
    first = []
    for c in range(cuts - 2):
        operands = [parts[c], second[c]] + ([near_last] if c == 1 else [])
        picked = call(pick_kernel, part, [VMEM] * len(operands), operands)
        first.append(permuted(picked, "blk", lambda i: i ^ 1))
    shape = jax.ShapeDtypeStruct(joint.shape, joint.dtype)
    picked = call(pick_kernel, shape, [VMEM] * 2, [joint, second[-1]])
    first.append(permuted(picked, "blk", lambda i: i ^ 1))
    sums = call(grams_kernel, grams, [VMEM] * (cuts - 1), [train] + first[:-1], work // 2)
    far = call(far_kernel, grams, [VMEM] * cuts, [train] + second, work)

    own = call(scores_kernel, rows, [VMEM] * (1 + cuts), [train] + parts, work)
    operands = [train, second_detour, second[-1], far]
    far = call(second_kernel, rows, [VMEM] * len(operands), operands, work // 4)
    sums = call(add_kernel, grams, [VMEM] * 4, [train, far_last, near_last, sums], 2 * work)
    out = jax.ShapeDtypeStruct((3,) + rows.shape, jnp.float32)
    operands = [train, first[-1], sums, own, far]
    partial_rows = call(last_kernel, out, [VMEM] * len(operands), operands, work // 4)
    return summed(partial_rows, "layer").transpose(2, 0, 1)


def solution(mesh):
    return jax.shard_map(
        local,
        mesh=mesh,
        in_specs=(P("blk", "layer", None, None, None), P("blk", "layer", None, None, None)),
        out_specs=P("blk", None, None),
        check_vma=False,
    )
```
